128 devices in a mesh: member: 8 (over y, x_lo), patch: 16 (over z, x_hi, core).
Axes of the slice: x: 4 (x_hi: 2, x_lo: 2; x = x_hi * 2 + x_lo), y: 4, z: 4, core: 2. Of those that a mesh axis runs over, the one named last changes fastest.
Arguments:
- fields: bfloat16 [128, 80, 64, 512], P(None, 'member', 'patch'), may hold values from -6 to 6
- block_device: int32 [128], replicated, may hold values from 0 to 127, each once
- weights: bfloat16 [128, 8, 80, 80], P(('member', 'patch')), may hold values from -0.3984375 to 1.59375
- control_increment: float32 [128, 64, 512], P(None, 'patch'), may hold values from -3 to 3
Outputs:
- analysis: bfloat16 [128, 80, 64, 512], P(None, 'member', 'patch')
The draws below stay inside these ranges and needn't reach their ends.
All inputs are finite; a program needn't handle non-finite values.
Results may differ from the reference program's by a relative error of at most 0.0054.
Values may be sent and summed in bfloat16 or wider, within the bound.
A program may use at most 128 MiB of HBM per device.

```python
import math
import jax
import jax.numpy as jnp
from jax import lax

K = 80
BW = 512
NLAT = 64
NPL = 8
DEVICES = 128


def draw_weights(key, part):
    key = jax.random.fold_in(key, 7)
    first_key, second_key = jax.random.split(key)
    shape = (DEVICES, NPL, K, K)
    offdiag = jax.random.normal(first_key, shape, jnp.float32) * (0.5 / math.sqrt(K))
    diagonal = jax.random.uniform(second_key, (DEVICES, NPL, K), jnp.float32, 0.6, 1.4)
    offdiag = jnp.clip(offdiag, -0.3984375, 0.3984375)
    rows_index = lax.broadcasted_iota(jnp.int32, (K, K), 0)
    cols_index = lax.broadcasted_iota(jnp.int32, (K, K), 1)
    identity = (rows_index == cols_index).astype(jnp.float32)
    result = offdiag * (1.0 - identity) + diagonal[..., None] * identity
    return result.astype(jnp.bfloat16)


def block_scale(stream_key, shape, pieces, low, top_value):
    factor_of, own = 1.0, jax.random.fold_in(stream_key, 6)
    for axis_at, parts in pieces:
        draws = jnp.exp(jax.random.uniform(jax.random.fold_in(own, axis_at), (parts,), jnp.float32, low / len(pieces), top_value / len(pieces)))
        factor_of = factor_of * jnp.repeat(draws, shape[axis_at] // parts).reshape([-1 if axis == axis_at else 1 for axis in range(len(shape))])
    return factor_of


def gaussian(rng, dims, spread, most, shards=(), kind=jnp.bfloat16):
    gain = block_scale(rng, dims, shards, -0.22, 0.18) if shards else 1.0
    values = jax.random.normal(rng, dims, jnp.float32) * spread * gain
    return jnp.minimum(jnp.maximum(values, -most), most).astype(kind)


def setup_inputs(seed: int = 0) -> dict:
    arg_keys = jax.random.split(jax.random.key(seed), 5)
    return {
        "fields": gaussian(arg_keys[0], (DEVICES, K, NLAT, BW), 1.0, 6.0, ((1, 8), (2, 16))),
        "block_device": jax.random.permutation(arg_keys[1], DEVICES).astype(jnp.int32),
        "weights": draw_weights(jax.random.fold_in(arg_keys[4], 71), 0),
        "control_increment": gaussian(arg_keys[3], (DEVICES, NLAT, BW), 0.5, 3.0, ((1, 16),), jnp.float32),
    }


RELAXATION = 0.85
EPSILON = 1e-06

def analyse(gathered, transform):
    members, rows, width = gathered.shape
    patches = transform.shape[0]
    values = gathered.astype(jnp.float32)
    prior_mean = lax.optimization_barrier(jnp.mean(values, axis=0))
    perturb = values - prior_mean
    prior_spread = lax.optimization_barrier(jnp.mean(perturb * perturb, axis=0))
    rounded = perturb.astype(jnp.bfloat16).reshape(members, patches, rows // patches, width)
    transformed = jnp.einsum('kqrc,qkj->jqrc', rounded.astype(jnp.float32), transform.astype(jnp.float32))
    transformed = transformed.reshape(members, rows, width)
    centered = transformed - lax.optimization_barrier(jnp.mean(transformed, axis=0))
    posterior_spread = lax.optimization_barrier(jnp.mean(centered * centered, axis=0))
    factor = RELAXATION * jnp.sqrt((prior_spread + EPSILON) / (posterior_spread + EPSILON)) + (1.0 - RELAXATION)
    return (prior_mean + factor * centered).astype(jnp.bfloat16)

def reference(fields, block_device, weights, control_increment):
    chosen = weights[block_device]
    results = lax.map(lambda pair: analyse(pair[0], pair[1]), (fields, chosen))
    return (results.astype(jnp.float32) + control_increment[:, None]).astype(jnp.bfloat16)
```

```python
import functools

import jax
import jax.numpy as jnp
from jax import lax
from jax.experimental import pallas as pl
from jax.experimental.pallas import tpu as pltpu
from jax.sharding import PartitionSpec as P

RELAXATION = 0.85
EPSILON = 1e-06
MESH = pl.DeviceIdType.MESH
LANES = 128


def wait_bytes(ref, sem):
    pltpu.make_async_copy(ref, ref, sem).wait()


def analyse(gathered, transform, control, pert, moved, result, members, rows):
    zero = jnp.zeros((rows, LANES), jnp.float32)

    def add(k, total):
        return total + gathered[k].astype(jnp.float32)

    prior_mean = lax.fori_loop(0, members, add, zero, unroll=8) / members

    def perturb(k, total):
        value = gathered[k].astype(jnp.float32) - prior_mean
        pert[pl.ds(pl.multiple_of(k * rows, rows), rows), :] = value
        return total + value * value

    prior_spread = lax.fori_loop(0, members, perturb, zero, unroll=8) / members

    out_in = transform.astype(jnp.float32).T.astype(jnp.bfloat16)
    for s in range(0, rows, 2):
        both = jnp.concatenate(
            [pert[pl.ds(s + i, members, stride=rows), :].astype(jnp.bfloat16) for i in range(2)],
            axis=1,
        )
        product = jnp.dot(out_in, both, preferred_element_type=jnp.float32)
        for i in range(2):
            moved[pl.ds(s + i, members, stride=rows), :] = product[:, i * LANES : (i + 1) * LANES]

    def at(j):
        return moved[pl.ds(pl.multiple_of(j * rows, rows), rows), :]

    post_mean = lax.fori_loop(0, members, lambda j, t: t + at(j), zero, unroll=8) / members

    def square(j, total):
        centered = at(j) - post_mean
        return total + centered * centered

    posterior_spread = lax.fori_loop(0, members, square, zero, unroll=8) / members
    factor = RELAXATION * jnp.sqrt((prior_spread + EPSILON) / (posterior_spread + EPSILON)) + (
        1.0 - RELAXATION
    )

    def write(j, carry):
        member = (prior_mean + factor * (at(j) - post_mean)).astype(jnp.bfloat16)
        result[j] = (member.astype(jnp.float32) + control).astype(jnp.bfloat16)
        return carry

    lax.fori_loop(0, members, write, 0, unroll=8)


def exchange(
    groups, bands, patches,
    owners, fields, weights, control,
    returned,
    held, ordered, gathered, result, chosen, increments, pert, moved,
    load_sem, weight_sems, gather_send, gather_recv, return_sems,
):
    blocks, local, rows, _ = held.shape
    mine = blocks // groups
    members = groups * local
    group = lax.axis_index("member")
    band = lax.axis_index("patch")
    load_fields = pltpu.make_async_copy(fields, held, load_sem.at[0])
    load_control = pltpu.make_async_copy(control, increments, load_sem.at[1])
    load_fields.start()
    load_control.start()

    def other_group(i):
        return lax.rem(group + i, groups)

    def other_band(i):
        return lax.rem(band + i, bands)

    barrier = pltpu.get_barrier_semaphore()

    def greet_group(i, carry):
        pl.semaphore_signal(barrier, inc=1, device_id=(other_group(i), band), device_id_type=MESH)
        return carry

    def greet_band(i, carry):
        pl.semaphore_signal(barrier, inc=1, device_id=(group, other_band(i)), device_id_type=MESH)
        return carry

    lax.fori_loop(1, groups, greet_group, 0)
    lax.fori_loop(1, bands, greet_band, 0)
    pl.semaphore_wait(barrier, groups + bands - 2)

    per_patch = bands // patches

    def send_weights(i, carry):
        to = other_band(i)
        pltpu.make_async_remote_copy(
            src_ref=weights.at[to // per_patch],
            dst_ref=chosen.at[band],
            send_sem=weight_sems.at[0],
            recv_sem=weight_sems.at[1],
            device_id=(group, to),
            device_id_type=MESH,
        ).start()
        return carry

    lax.fori_loop(1, bands, send_weights, 0)
    own_weights = pltpu.make_async_copy(
        weights.at[band // per_patch], chosen.at[band], weight_sems.at[2]
    )
    own_weights.start()

    load_fields.wait()

    def send_block(c, carry):
        here = owners[group * mine + c]
        for k in range(local):
            gathered[c, group * local + k] = held[here, k]

        def to_peer(i, inner):
            to = other_group(i)
            block = owners[to * mine + c]
            for k in range(local):
                ordered[i - 1, c, k] = held[block, k]
            pltpu.make_async_remote_copy(
                src_ref=ordered.at[i - 1, c],
                dst_ref=gathered.at[c, pl.ds(group * local, local)],
                send_sem=gather_send,
                recv_sem=gather_recv.at[c],
                device_id=(to, band),
                device_id_type=MESH,
            ).start()
            return inner

        lax.fori_loop(1, groups, to_peer, 0)
        return carry

    lax.fori_loop(0, mine, send_block, 0)

    load_control.wait()
    own_weights.wait()
    wait_bytes(chosen.at[pl.ds(0, bands - 1)], weight_sems.at[1])

    def analyse_block(c, carry):
        wait_bytes(gathered.at[c, pl.ds(0, members - local)], gather_recv.at[c])
        slot = group * mine + c
        analyse(
            gathered.at[c], chosen[c], increments[owners[slot]],
            pert, moved, result.at[c], members, rows,
        )

        def to_peer(i, inner):
            to = other_group(i)
            pltpu.make_async_remote_copy(
                src_ref=result.at[c, pl.ds(to * local, local)],
                dst_ref=returned.at[slot],
                send_sem=return_sems.at[0],
                recv_sem=return_sems.at[1],
                device_id=(to, band),
                device_id_type=MESH,
            ).start()
            return inner

        lax.fori_loop(1, groups, to_peer, 0)
        pltpu.make_async_copy(
            result.at[c, pl.ds(group * local, local)], returned.at[slot], return_sems.at[2]
        ).start()
        return carry

    lax.fori_loop(0, mine, analyse_block, 0)

    sent = returned.at[pl.ds(0, blocks - mine)]
    wait_bytes(sent, return_sems.at[1])
    wait_bytes(returned.at[pl.ds(0, mine)], return_sems.at[2])
    wait_bytes(chosen.at[pl.ds(0, bands - 1)], weight_sems.at[0])
    wait_bytes(ordered, gather_send)
    wait_bytes(sent, return_sems.at[0])


def place(block_device, returned, analysis, sem):
    blocks = returned.shape[0]

    def one(b, carry):
        pltpu.make_async_copy(returned.at[block_device[b]], analysis.at[b], sem).start()
        return carry

    lax.fori_loop(0, blocks, one, 0)
    wait_bytes(returned, sem)


def per_device(groups, bands, fields, block_device, weights, control_increment):
    blocks, local, band_rows, width = fields.shape
    patches, members = weights.shape[1], weights.shape[2]
    pieces = width // LANES
    rows = pieces * band_rows
    tiled = (
        fields.reshape(blocks, local, band_rows, pieces, LANES)
        .transpose(0, 1, 3, 2, 4)
        .reshape(blocks, local, rows, LANES)
    )
    control = (
        control_increment.reshape(blocks, band_rows, pieces, LANES)
        .transpose(0, 2, 1, 3)
        .reshape(blocks, rows, LANES)
    )
    index = jnp.arange(blocks, dtype=jnp.int32)
    owners = jnp.sum(
        jnp.where(block_device[None, :] == index[:, None], index[None, :], 0), axis=1
    ).astype(jnp.int32)
    mine = blocks // groups
    any_space = pl.BlockSpec(memory_space=pl.ANY)
    smem = pl.BlockSpec(memory_space=pltpu.SMEM)
    half = jnp.bfloat16
    returned = pl.pallas_call(
        functools.partial(exchange, groups, bands, patches),
        out_shape=jax.ShapeDtypeStruct((blocks, local, rows, LANES), half),
        in_specs=[smem, any_space, any_space, any_space],
        out_specs=any_space,
        scratch_shapes=[
            pltpu.VMEM((blocks, local, rows, LANES), half),
            pltpu.VMEM((groups - 1, mine, local, rows, LANES), half),
            pltpu.VMEM((mine, members, rows, LANES), half),
            pltpu.VMEM((mine, members, rows, LANES), half),
            pltpu.VMEM((bands, members, members), half),
            pltpu.VMEM((blocks, rows, LANES), jnp.float32),
            pltpu.VMEM((members * rows, LANES), jnp.float32),
            pltpu.VMEM((members * rows, LANES), jnp.float32),
            pltpu.SemaphoreType.DMA((2,)),
            pltpu.SemaphoreType.DMA((3,)),
            pltpu.SemaphoreType.DMA,
            pltpu.SemaphoreType.DMA((mine,)),
            pltpu.SemaphoreType.DMA((3,)),
        ],
        compiler_params=pltpu.CompilerParams(
            collective_id=0, has_side_effects=True, vmem_limit_bytes=48 * 2**20
        ),
        name="exchange",
    )(owners, tiled, weights[0], control)
    analysis = pl.pallas_call(
        place,
        out_shape=jax.ShapeDtypeStruct((blocks, local, rows, LANES), half),
        in_specs=[smem, any_space],
        out_specs=any_space,
        scratch_shapes=[pltpu.SemaphoreType.DMA],
        name="place",
    )(block_device, returned)
    return (
        analysis.reshape(blocks, local, pieces, band_rows, LANES)
        .transpose(0, 1, 3, 2, 4)
        .reshape(blocks, local, band_rows, width)
    )


def solution(mesh):
    return jax.shard_map(
        functools.partial(per_device, mesh.shape["member"], mesh.shape["patch"]),
        mesh=mesh,
        in_specs=(
            P(None, "member", "patch", None),
            P(),
            P(("member", "patch"), None, None, None),
            P(None, "patch", None),
        ),
        out_specs=P(None, "member", "patch", None),
        check_vma=False,
    )
```

```python
import functools

import jax
import jax.numpy as jnp
from jax import lax
from jax.experimental import pallas as pl
from jax.experimental.pallas import tpu as pltpu
from jax.sharding import PartitionSpec as P

RELAXATION = 0.85
EPSILON = 1e-06
MESH = pl.DeviceIdType.MESH
LANES = 128


def wait_bytes(ref, sem):
    pltpu.make_async_copy(ref, ref, sem).wait()


def analyse(gathered, transform, control, pert, moved, result, members, rows):
    zero = jnp.zeros((rows, LANES), jnp.float32)

    def add(k, total):
        return total + gathered[k].astype(jnp.float32)

    prior_mean = lax.fori_loop(0, members, add, zero, unroll=8) / members

    def perturb(k, total):
        value = gathered[k].astype(jnp.float32) - prior_mean
        pert[pl.ds(pl.multiple_of(k * rows, rows), rows), :] = value
        return total + value * value

    prior_spread = lax.fori_loop(0, members, perturb, zero, unroll=8) / members

    out_in = transform.astype(jnp.float32).T.astype(jnp.bfloat16)
    for s in range(0, rows, 2):
        both = jnp.concatenate(
            [pert[pl.ds(s + i, members, stride=rows), :].astype(jnp.bfloat16) for i in range(2)],
            axis=1,
        )
        product = jnp.dot(out_in, both, preferred_element_type=jnp.float32)
        for i in range(2):
            moved[pl.ds(s + i, members, stride=rows), :] = product[:, i * LANES : (i + 1) * LANES]

    def at(j):
        return moved[pl.ds(pl.multiple_of(j * rows, rows), rows), :]

    post_mean = lax.fori_loop(0, members, lambda j, t: t + at(j), zero, unroll=8) / members

    def square(j, total):
        centered = at(j) - post_mean
        return total + centered * centered

    posterior_spread = lax.fori_loop(0, members, square, zero, unroll=8) / members
    factor = RELAXATION * jnp.sqrt((prior_spread + EPSILON) / (posterior_spread + EPSILON)) + (
        1.0 - RELAXATION
    )

    def write(j, carry):
        member = (prior_mean + factor * (at(j) - post_mean)).astype(jnp.bfloat16)
        result[j] = (member.astype(jnp.float32) + control).astype(jnp.bfloat16)
        return carry

    lax.fori_loop(0, members, write, 0, unroll=8)


def exchange(
    groups, bands, patches,
    block_device, fields, weights, control,
    returned,
    held, ordered, gathered, result, chosen, increments, pert, moved, owner_row, owners,
    load_sems, weight_sems, gather_send, gather_recv, return_sems,
):
    blocks, local, rows, _ = held.shape
    mine = blocks // groups
    members = groups * local
    group = lax.axis_index("member")
    band = lax.axis_index("patch")
    parts = 4

    def load_fields(i):
        part = pl.ds(i * (blocks // parts), blocks // parts)
        return pltpu.make_async_copy(fields.at[part], held.at[part], load_sems.at[2 + i])

    load_control = pltpu.make_async_copy(control, increments, load_sems.at[0])
    for i in range(parts):
        load_fields(i).start()

    def other_group(i):
        return lax.rem(group + i, groups)

    def half(of_band):
        return lax.rem(of_band // 2, 2)

    def weights_peer(i):
        to = lax.rem(band + i, bands)
        return group // 2 * 2 + lax.rem(group + half(band) + half(to), 2), to

    def slot_of(to, i):
        return (to // 2 * 2 + lax.rem(to + half(band) + half(i), 2)) * bands + i

    barrier = pltpu.get_barrier_semaphore()

    def greet_group(i, carry):
        pl.semaphore_signal(barrier, inc=1, device_id=(other_group(i), band), device_id_type=MESH)
        return carry

    def greet_band(i, carry):
        pl.semaphore_signal(barrier, inc=1, device_id=weights_peer(i), device_id_type=MESH)
        return carry

    lax.fori_loop(1, groups, greet_group, 0)
    lax.fori_loop(1, bands, greet_band, 0)

    shape = (blocks, blocks)
    match = block_device[...] == lax.broadcasted_iota(jnp.int32, shape, 0)
    index = jnp.where(match, lax.broadcasted_iota(jnp.int32, shape, 1), 0)
    owner_row[...] = jnp.max(index.T, axis=0, keepdims=True)
    load_owners = pltpu.make_async_copy(owner_row, owners, load_sems.at[1])
    load_owners.start()

    pl.semaphore_wait(barrier, groups + bands - 2)

    per_patch = bands // patches

    def send_weights(i, carry):
        to = weights_peer(i)
        pltpu.make_async_remote_copy(
            src_ref=weights.at[to[1] // per_patch],
            dst_ref=chosen.at[band],
            send_sem=weight_sems.at[0],
            recv_sem=weight_sems.at[1],
            device_id=to,
            device_id_type=MESH,
        ).start()
        return carry

    lax.fori_loop(1, bands, send_weights, 0)
    own_weights = pltpu.make_async_copy(
        weights.at[band // per_patch], chosen.at[band], weight_sems.at[2]
    )
    own_weights.start()

    load_owners.wait()
    for i in range(parts):
        load_fields(i).wait()
    load_control.start()

    def send_block(c, carry):
        here = owners[0, slot_of(group, c)]
        for k in range(local):
            gathered[c, group * local + k] = held[here, k]

        def to_peer(i, inner):
            to = other_group(i)
            block = owners[0, slot_of(to, c)]
            for k in range(local):
                ordered[i - 1, c, k] = held[block, k]
            pltpu.make_async_remote_copy(
                src_ref=ordered.at[i - 1, c],
                dst_ref=gathered.at[c, pl.ds(group * local, local)],
                send_sem=gather_send,
                recv_sem=gather_recv.at[c],
                device_id=(to, band),
                device_id_type=MESH,
            ).start()
            return inner

        lax.fori_loop(1, groups, to_peer, 0)
        return carry

    lax.fori_loop(0, mine, send_block, 0)

    load_control.wait()
    own_weights.wait()
    wait_bytes(chosen.at[pl.ds(0, bands - 1)], weight_sems.at[1])

    def analyse_block(c, carry):
        wait_bytes(gathered.at[c, pl.ds(0, members - local)], gather_recv.at[c])
        slot = slot_of(group, c)
        analyse(
            gathered.at[c], chosen[c], increments[owners[0, slot]],
            pert, moved, result.at[c], members, rows,
        )

        def to_peer(i, inner):
            to = other_group(i)
            pltpu.make_async_remote_copy(
                src_ref=result.at[c, pl.ds(to * local, local)],
                dst_ref=returned.at[slot],
                send_sem=return_sems.at[0],
                recv_sem=return_sems.at[1],
                device_id=(to, band),
                device_id_type=MESH,
            ).start()
            return inner

        lax.fori_loop(1, groups, to_peer, 0)
        for k in range(local):
            returned[slot, k] = result[c, group * local + k]
        return carry

    lax.fori_loop(0, mine, analyse_block, 0)

    sent = returned.at[pl.ds(0, blocks - mine)]
    wait_bytes(sent, return_sems.at[1])
    wait_bytes(chosen.at[pl.ds(0, bands - 1)], weight_sems.at[0])
    wait_bytes(ordered, gather_send)
    wait_bytes(sent, return_sems.at[0])


def place(block_device, returned, analysis, sem):
    for b in range(returned.shape[0]):
        pltpu.make_async_copy(returned.at[block_device[b]], analysis.at[b], sem).start()
    wait_bytes(returned, sem)


def per_device(groups, bands, fields, block_device, weights, control_increment):
    blocks, local, band_rows, width = fields.shape
    patches, members = weights.shape[1], weights.shape[2]
    pieces = width // LANES
    rows = pieces * band_rows
    tiled = (
        fields.reshape(blocks, local, band_rows, pieces, LANES)
        .transpose(0, 1, 3, 2, 4)
        .reshape(blocks, local, rows, LANES)
    )
    control = (
        control_increment.reshape(blocks, band_rows, pieces, LANES)
        .transpose(0, 2, 1, 3)
        .reshape(blocks, rows, LANES)
    )
    mine = blocks // groups
    any_space = pl.BlockSpec(memory_space=pl.ANY)
    smem = pl.BlockSpec(memory_space=pltpu.SMEM)
    half = jnp.bfloat16
    returned = pl.pallas_call(
        functools.partial(exchange, groups, bands, patches),
        out_shape=pltpu.VMEM((blocks, local, rows, LANES), half),
        in_specs=[pl.BlockSpec(memory_space=pltpu.VMEM)] + [pl.BlockSpec(memory_space=pltpu.HBM)] * 3,
        out_specs=pl.BlockSpec(memory_space=pltpu.VMEM),
        scratch_shapes=[
            pltpu.VMEM((blocks, local, rows, LANES), half),
            pltpu.VMEM((groups - 1, mine, local, rows, LANES), half),
            pltpu.VMEM((mine, members, rows, LANES), half),
            pltpu.VMEM((mine, members, rows, LANES), half),
            pltpu.VMEM((bands, members, members), half),
            pltpu.VMEM((blocks, rows, LANES), jnp.float32),
            pltpu.VMEM((members * rows, LANES), jnp.float32),
            pltpu.VMEM((members * rows, LANES), jnp.float32),
            pltpu.VMEM((1, blocks), jnp.int32),
            pltpu.SMEM((1, blocks), jnp.int32),
            pltpu.SemaphoreType.DMA((6,)),
            pltpu.SemaphoreType.DMA((3,)),
            pltpu.SemaphoreType.DMA,
            pltpu.SemaphoreType.DMA((mine,)),
            pltpu.SemaphoreType.DMA((2,)),
        ],
        compiler_params=pltpu.CompilerParams(
            collective_id=0, has_side_effects=True, vmem_limit_bytes=58 * 2**20
        ),
        name="exchange",
    )(block_device.reshape(1, blocks), tiled, weights[0], control)
    steps = 8
    analysis = pl.pallas_call(
        place,
        out_shape=jax.ShapeDtypeStruct((blocks, local, rows, LANES), half),
        in_specs=[smem, any_space],
        out_specs=any_space,
        scratch_shapes=[pltpu.SemaphoreType.DMA],
        compiler_params=pltpu.CompilerParams(vmem_limit_bytes=8 * 2**20),
        name="place",
    )(block_device, returned)
    return (
        analysis.reshape(blocks, local, pieces, band_rows, LANES)
        .transpose(0, 1, 3, 2, 4)
        .reshape(blocks, local, band_rows, width)
    )


def solution(mesh):
    return jax.shard_map(
        functools.partial(per_device, mesh.shape["member"], mesh.shape["patch"]),
        mesh=mesh,
        in_specs=(
            P(None, "member", "patch", None),
            P(),
            P(("member", "patch"), None, None, None),
            P(None, "patch", None),
        ),
        out_specs=P(None, "member", "patch", None),
        check_vma=False,
    )
```

```python
import functools

import jax
import jax.numpy as jnp
from jax import lax
from jax.experimental import pallas as pl
from jax.experimental.pallas import tpu as pltpu
from jax.sharding import PartitionSpec as P

RELAXATION = 0.85
EPSILON = 1e-06
MESH = pl.DeviceIdType.MESH
LANES = 128


def wait_bytes(ref, sem):
    pltpu.make_async_copy(ref, ref, sem).wait()


def analyse(gathered, transform, control, pert, moved, result, members, rows):
    zero = jnp.zeros((rows, LANES), jnp.float32)

    def add(k, total):
        return total + gathered[k].astype(jnp.float32)

    prior_mean = lax.fori_loop(0, members, add, zero, unroll=8) / members

    def perturb(k, total):
        value = gathered[k].astype(jnp.float32) - prior_mean
        pert[pl.ds(pl.multiple_of(k * rows, rows), rows), :] = value
        return total + value * value

    prior_spread = lax.fori_loop(0, members, perturb, zero, unroll=8) / members

    out_in = transform.astype(jnp.float32).T.astype(jnp.bfloat16)
    for s in range(0, rows, 2):
        both = jnp.concatenate(
            [pert[pl.ds(s + i, members, stride=rows), :].astype(jnp.bfloat16) for i in range(2)],
            axis=1,
        )
        product = jnp.dot(out_in, both, preferred_element_type=jnp.float32)
        for i in range(2):
            moved[pl.ds(s + i, members, stride=rows), :] = product[:, i * LANES : (i + 1) * LANES]

    def at(j):
        return moved[pl.ds(pl.multiple_of(j * rows, rows), rows), :]

    post_mean = lax.fori_loop(0, members, lambda j, t: t + at(j), zero, unroll=8) / members

    def square(j, total):
        centered = at(j) - post_mean
        return total + centered * centered

    posterior_spread = lax.fori_loop(0, members, square, zero, unroll=8) / members
    factor = RELAXATION * jnp.sqrt((prior_spread + EPSILON) / (posterior_spread + EPSILON)) + (
        1.0 - RELAXATION
    )

    def write(j, carry):
        member = (prior_mean + factor * (at(j) - post_mean)).astype(jnp.bfloat16)
        result[j] = (member.astype(jnp.float32) + control).astype(jnp.bfloat16)
        return carry

    lax.fori_loop(0, members, write, 0, unroll=8)


def exchange(
    groups, bands, patches,
    block_device, fields, weights, control,
    returned,
    held, ordered, gathered, result, chosen, increments, pert, moved, owner_row, owners,
    load_sems, weight_sems, gather_send, gather_recv, return_sems, later,
):
    blocks, local, rows, _ = held.shape
    mine = blocks // groups
    members = groups * local
    group = lax.axis_index("member")
    band = lax.axis_index("patch")
    parts = 4

    def load_fields(i):
        part = pl.ds(i * (blocks // parts), blocks // parts)
        return pltpu.make_async_copy(fields.at[part], held.at[part], load_sems.at[2 + i])

    load_control = pltpu.make_async_copy(control, increments, load_sems.at[0])
    for i in range(parts):
        load_fields(i).start()

    def other_group(i):
        return lax.rem(group + i, groups)

    def half(of_band):
        return lax.rem(of_band // 2, 2)

    def weights_peer(to):
        return group // 2 * 2 + lax.rem(group + half(band) + half(to), 2), to

    def slot_of(to, i):
        return (to // 2 * 2 + lax.rem(to + half(band) + half(i), 2)) * bands + i

    barrier = pltpu.get_barrier_semaphore()

    def greet_group(i, carry):
        pl.semaphore_signal(barrier, inc=1, device_id=(other_group(i), band), device_id_type=MESH)
        return carry

    def greet_later(to, carry):
        pl.semaphore_signal(barrier, inc=1, device_id=weights_peer(to), device_id_type=MESH)
        return carry

    def greet_earlier(to, carry):
        pl.semaphore_signal(later, inc=1, device_id=weights_peer(to), device_id_type=MESH)
        return carry

    lax.fori_loop(1, groups, greet_group, 0)
    lax.fori_loop(band + 1, bands, greet_later, 0)

    shape = (blocks, blocks)
    match = block_device[...] == lax.broadcasted_iota(jnp.int32, shape, 0)
    index = jnp.where(match, lax.broadcasted_iota(jnp.int32, shape, 1), 0)
    owner_row[...] = jnp.max(index.T, axis=0, keepdims=True)
    load_owners = pltpu.make_async_copy(owner_row, owners, load_sems.at[1])
    load_owners.start()

    pl.semaphore_wait(barrier, groups - 1 + band)
    lax.fori_loop(0, band, greet_earlier, 0)

    per_patch = bands // patches

    def send_weights(to, carry):
        pltpu.make_async_remote_copy(
            src_ref=weights.at[to // per_patch],
            dst_ref=chosen.at[band],
            send_sem=weight_sems.at[0],
            recv_sem=weight_sems.at[1],
            device_id=weights_peer(to),
            device_id_type=MESH,
        ).start()
        return carry

    lax.fori_loop(0, band, send_weights, 0)
    own_weights = pltpu.make_async_copy(
        weights.at[band // per_patch], chosen.at[band], weight_sems.at[2]
    )
    own_weights.start()

    load_owners.wait()
    for i in range(parts):
        load_fields(i).wait()
    load_control.start()

    def send_block(c, carry):
        here = owners[0, slot_of(group, c)]
        for k in range(local):
            gathered[c, group * local + k] = held[here, k]

        def to_peer(i, inner):
            to = other_group(i)
            block = owners[0, slot_of(to, c)]
            for k in range(local):
                ordered[i - 1, c, k] = held[block, k]
            pltpu.make_async_remote_copy(
                src_ref=ordered.at[i - 1, c],
                dst_ref=gathered.at[c, pl.ds(group * local, local)],
                send_sem=gather_send,
                recv_sem=gather_recv.at[c],
                device_id=(to, band),
                device_id_type=MESH,
            ).start()
            return inner

        lax.fori_loop(1, groups, to_peer, 0)
        return carry

    lax.fori_loop(0, 2, send_block, 0)

    @pl.when(band < bands - 1)
    def _():
        pl.semaphore_wait(later, bands - 1 - band)

    lax.fori_loop(band + 1, bands, send_weights, 0)
    lax.fori_loop(2, mine, send_block, 0)

    load_control.wait()
    own_weights.wait()
    wait_bytes(chosen.at[pl.ds(0, bands - 1)], weight_sems.at[1])

    def analyse_block(c, carry):
        wait_bytes(gathered.at[c, pl.ds(0, members - local)], gather_recv.at[c])
        slot = slot_of(group, c)
        analyse(
            gathered.at[c], chosen[c], increments[owners[0, slot]],
            pert, moved, result.at[c], members, rows,
        )

        def to_peer(i, inner):
            to = other_group(i)
            pltpu.make_async_remote_copy(
                src_ref=result.at[c, pl.ds(to * local, local)],
                dst_ref=returned.at[slot],
                send_sem=return_sems.at[0],
                recv_sem=return_sems.at[1],
                device_id=(to, band),
                device_id_type=MESH,
            ).start()
            return inner

        lax.fori_loop(1, groups, to_peer, 0)
        for k in range(local):
            returned[slot, k] = result[c, group * local + k]
        return carry

    lax.fori_loop(0, mine, analyse_block, 0)

    sent = returned.at[pl.ds(0, blocks - mine)]
    wait_bytes(sent, return_sems.at[1])
    wait_bytes(chosen.at[pl.ds(0, bands - 1)], weight_sems.at[0])
    wait_bytes(ordered, gather_send)
    wait_bytes(sent, return_sems.at[0])


def place(block_device, returned, analysis, sem):
    for b in range(returned.shape[0]):
        pltpu.make_async_copy(returned.at[block_device[b]], analysis.at[b], sem).start()
    wait_bytes(returned, sem)


def per_device(groups, bands, fields, block_device, weights, control_increment):
    blocks, local, band_rows, width = fields.shape
    patches, members = weights.shape[1], weights.shape[2]
    pieces = width // LANES
    rows = pieces * band_rows
    tiled = (
        fields.reshape(blocks, local, band_rows, pieces, LANES)
        .transpose(0, 1, 3, 2, 4)
        .reshape(blocks, local, rows, LANES)
    )
    control = (
        control_increment.reshape(blocks, band_rows, pieces, LANES)
        .transpose(0, 2, 1, 3)
        .reshape(blocks, rows, LANES)
    )
    mine = blocks // groups
    any_space = pl.BlockSpec(memory_space=pl.ANY)
    smem = pl.BlockSpec(memory_space=pltpu.SMEM)
    half = jnp.bfloat16
    returned = pl.pallas_call(
        functools.partial(exchange, groups, bands, patches),
        out_shape=pltpu.VMEM((blocks, local, rows, LANES), half),
        in_specs=[pl.BlockSpec(memory_space=pltpu.VMEM)] + [pl.BlockSpec(memory_space=pltpu.HBM)] * 3,
        out_specs=pl.BlockSpec(memory_space=pltpu.VMEM),
        scratch_shapes=[
            pltpu.VMEM((blocks, local, rows, LANES), half),
            pltpu.VMEM((groups - 1, mine, local, rows, LANES), half),
            pltpu.VMEM((mine, members, rows, LANES), half),
            pltpu.VMEM((mine, members, rows, LANES), half),
            pltpu.VMEM((bands, members, members), half),
            pltpu.VMEM((blocks, rows, LANES), jnp.float32),
            pltpu.VMEM((members * rows, LANES), jnp.float32),
            pltpu.VMEM((members * rows, LANES), jnp.float32),
            pltpu.VMEM((1, blocks), jnp.int32),
            pltpu.SMEM((1, blocks), jnp.int32),
            pltpu.SemaphoreType.DMA((6,)),
            pltpu.SemaphoreType.DMA((3,)),
            pltpu.SemaphoreType.DMA,
            pltpu.SemaphoreType.DMA((mine,)),
            pltpu.SemaphoreType.DMA((2,)),
            pltpu.SemaphoreType.REGULAR,
        ],
        compiler_params=pltpu.CompilerParams(
            collective_id=0, has_side_effects=True, vmem_limit_bytes=58 * 2**20
        ),
        name="exchange",
    )(block_device.reshape(1, blocks), tiled, weights[0], control)
    steps = 8
    analysis = pl.pallas_call(
        place,
        out_shape=jax.ShapeDtypeStruct((blocks, local, rows, LANES), half),
        in_specs=[smem, any_space],
        out_specs=any_space,
        scratch_shapes=[pltpu.SemaphoreType.DMA],
        compiler_params=pltpu.CompilerParams(vmem_limit_bytes=8 * 2**20),
        name="place",
    )(block_device, returned)
    return (
        analysis.reshape(blocks, local, pieces, band_rows, LANES)
        .transpose(0, 1, 3, 2, 4)
        .reshape(blocks, local, band_rows, width)
    )


def solution(mesh):
    return jax.shard_map(
        functools.partial(per_device, mesh.shape["member"], mesh.shape["patch"]),
        mesh=mesh,
        in_specs=(
            P(None, "member", "patch", None),
            P(),
            P(("member", "patch"), None, None, None),
            P(None, "patch", None),
        ),
        out_specs=P(None, "member", "patch", None),
        check_vma=False,
    )
```

```python
import functools

import jax
import jax.numpy as jnp
from jax import lax
from jax.experimental import pallas as pl
from jax.experimental.pallas import tpu as pltpu
from jax.sharding import PartitionSpec as P

RELAXATION = 0.85
EPSILON = 1e-06
MESH = pl.DeviceIdType.MESH
LANES = 128


def wait_bytes(ref, sem):
    pltpu.make_async_copy(ref, ref, sem).wait()


def analyse(gathered, transform, control, pert, moved, result, members, rows):
    zero = jnp.zeros((rows, LANES), jnp.float32)

    def add(k, total):
        return total + gathered[k].astype(jnp.float32)

    prior_mean = lax.fori_loop(0, members, add, zero, unroll=8) / members

    def perturb(k, total):
        value = gathered[k].astype(jnp.float32) - prior_mean
        pert[pl.ds(pl.multiple_of(k * rows, rows), rows), :] = value
        return total + value * value

    prior_spread = lax.fori_loop(0, members, perturb, zero, unroll=8) / members

    out_in = transform.astype(jnp.float32).T.astype(jnp.bfloat16)
    for s in range(0, rows, 2):
        both = jnp.concatenate(
            [pert[pl.ds(s + i, members, stride=rows), :].astype(jnp.bfloat16) for i in range(2)],
            axis=1,
        )
        product = jnp.dot(out_in, both, preferred_element_type=jnp.float32)
        for i in range(2):
            moved[pl.ds(s + i, members, stride=rows), :] = product[:, i * LANES : (i + 1) * LANES]

    def at(j):
        return moved[pl.ds(pl.multiple_of(j * rows, rows), rows), :]

    post_mean = lax.fori_loop(0, members, lambda j, t: t + at(j), zero, unroll=8) / members

    def square(j, total):
        centered = at(j) - post_mean
        return total + centered * centered

    posterior_spread = lax.fori_loop(0, members, square, zero, unroll=8) / members
    factor = RELAXATION * jnp.sqrt((prior_spread + EPSILON) / (posterior_spread + EPSILON)) + (
        1.0 - RELAXATION
    )

    def write(j, carry):
        member = (prior_mean + factor * (at(j) - post_mean)).astype(jnp.bfloat16)
        result[j] = (member.astype(jnp.float32) + control).astype(jnp.bfloat16)
        return carry

    lax.fori_loop(0, members, write, 0, unroll=8)


def exchange(
    groups, bands, patches,
    block_device, fields, weights, control,
    returned,
    held, ordered, gathered, result, chosen, increments, pert, moved, devices, owner_row, owners,
    load_sems, weight_sems, gather_send, gather_recv, return_sems, later,
):
    blocks, local, rows, _ = held.shape
    mine = blocks // groups
    members = groups * local
    group = lax.axis_index("member")
    band = lax.axis_index("patch")
    parts = 4

    def load_fields(i):
        part = pl.ds(i * (blocks // parts), blocks // parts)
        return pltpu.make_async_copy(fields.at[part], held.at[part], load_sems.at[2 + i])

    load_control = pltpu.make_async_copy(control, increments, load_sems.at[0])

    def other_group(i):
        return lax.rem(group + i, groups)

    def half(of_band):
        return lax.rem(of_band // 2, 2)

    def weights_peer(to):
        return group // 2 * 2 + lax.rem(group + half(band) + half(to), 2), to

    def slot_of(to, i):
        return (to // 2 * 2 + lax.rem(to + half(band) + half(i), 2)) * bands + i

    barrier = pltpu.get_barrier_semaphore()

    def greet_group(i, carry):
        pl.semaphore_signal(barrier, inc=1, device_id=(other_group(i), band), device_id_type=MESH)
        return carry

    def greet_later(to, carry):
        pl.semaphore_signal(barrier, inc=1, device_id=weights_peer(to), device_id_type=MESH)
        return carry

    def greet_earlier(to, carry):
        pl.semaphore_signal(later, inc=1, device_id=weights_peer(to), device_id_type=MESH)
        return carry

    lax.fori_loop(1, groups, greet_group, 0)
    load_devices = pltpu.make_async_copy(block_device, devices, load_sems.at[1])
    load_devices.start()
    for i in range(parts):
        load_fields(i).start()
    lax.fori_loop(band + 1, bands, greet_later, 0)

    load_devices.wait()
    shape = (blocks, blocks)
    match = devices[...] == lax.broadcasted_iota(jnp.int32, shape, 0)
    index = jnp.where(match, lax.broadcasted_iota(jnp.int32, shape, 1), 0)
    owner_row[...] = jnp.max(index.T, axis=0, keepdims=True)
    load_owners = pltpu.make_async_copy(owner_row, owners, load_sems.at[1])
    load_owners.start()

    pl.semaphore_wait(barrier, groups - 1 + band)

    per_patch = bands // patches

    def send_weights(to, carry):
        pltpu.make_async_remote_copy(
            src_ref=weights.at[to // per_patch],
            dst_ref=chosen.at[band],
            send_sem=weight_sems.at[0],
            recv_sem=weight_sems.at[1],
            device_id=weights_peer(to),
            device_id_type=MESH,
        ).start()
        return carry

    own_weights = pltpu.make_async_copy(
        weights.at[band // per_patch], chosen.at[band], weight_sems.at[2]
    )
    own_weights.start()

    load_owners.wait()
    for i in range(parts):
        load_fields(i).wait()
    load_control.start()

    def send_block(c, carry):
        here = owners[0, slot_of(group, c)]
        for k in range(local):
            gathered[c, group * local + k] = held[here, k]

        def to_peer(i, inner):
            to = other_group(i)
            block = owners[0, slot_of(to, c)]
            for k in range(local):
                ordered[i - 1, c, k] = held[block, k]
            pltpu.make_async_remote_copy(
                src_ref=ordered.at[i - 1, c],
                dst_ref=gathered.at[c, pl.ds(group * local, local)],
                send_sem=gather_send,
                recv_sem=gather_recv.at[c],
                device_id=(to, band),
                device_id_type=MESH,
            ).start()
            return inner

        lax.fori_loop(1, groups, to_peer, 0)
        return carry

    lax.fori_loop(0, 1, send_block, 0)
    lax.fori_loop(0, band, greet_earlier, 0)
    lax.fori_loop(0, band, send_weights, 0)
    lax.fori_loop(1, 2, send_block, 0)

    @pl.when(band < bands - 1)
    def _():
        pl.semaphore_wait(later, bands - 1 - band)

    lax.fori_loop(band + 1, bands, send_weights, 0)
    lax.fori_loop(2, mine, send_block, 0)

    load_control.wait()
    own_weights.wait()
    wait_bytes(chosen.at[pl.ds(0, bands - 1)], weight_sems.at[1])

    def analyse_block(c, carry):
        wait_bytes(gathered.at[c, pl.ds(0, members - local)], gather_recv.at[c])
        slot = slot_of(group, c)
        analyse(
            gathered.at[c], chosen[c], increments[owners[0, slot]],
            pert, moved, result.at[c], members, rows,
        )

        def to_peer(i, inner):
            to = other_group(i)
            pltpu.make_async_remote_copy(
                src_ref=result.at[c, pl.ds(to * local, local)],
                dst_ref=returned.at[slot],
                send_sem=return_sems.at[0],
                recv_sem=return_sems.at[1],
                device_id=(to, band),
                device_id_type=MESH,
            ).start()
            return inner

        lax.fori_loop(1, groups, to_peer, 0)
        for k in range(local):
            returned[slot, k] = result[c, group * local + k]
        return carry

    lax.fori_loop(0, mine, analyse_block, 0)

    sent = returned.at[pl.ds(0, blocks - mine)]
    wait_bytes(sent, return_sems.at[1])
    wait_bytes(chosen.at[pl.ds(0, bands - 1)], weight_sems.at[0])
    wait_bytes(ordered, gather_send)
    wait_bytes(sent, return_sems.at[0])


def place(block_device, returned, analysis, sem):
    for b in range(returned.shape[0]):
        pltpu.make_async_copy(returned.at[block_device[b]], analysis.at[b], sem).start()
    wait_bytes(returned, sem)


def per_device(groups, bands, fields, block_device, weights, control_increment):
    blocks, local, band_rows, width = fields.shape
    patches, members = weights.shape[1], weights.shape[2]
    pieces = width // LANES
    rows = pieces * band_rows
    tiled = (
        fields.reshape(blocks, local, band_rows, pieces, LANES)
        .transpose(0, 1, 3, 2, 4)
        .reshape(blocks, local, rows, LANES)
    )
    control = (
        control_increment.reshape(blocks, band_rows, pieces, LANES)
        .transpose(0, 2, 1, 3)
        .reshape(blocks, rows, LANES)
    )
    mine = blocks // groups
    any_space = pl.BlockSpec(memory_space=pl.ANY)
    smem = pl.BlockSpec(memory_space=pltpu.SMEM)
    half = jnp.bfloat16
    returned = pl.pallas_call(
        functools.partial(exchange, groups, bands, patches),
        out_shape=pltpu.VMEM((blocks, local, rows, LANES), half),
        in_specs=[pl.BlockSpec(memory_space=pltpu.HBM)] * 4,
        out_specs=pl.BlockSpec(memory_space=pltpu.VMEM),
        scratch_shapes=[
            pltpu.VMEM((blocks, local, rows, LANES), half),
            pltpu.VMEM((groups - 1, mine, local, rows, LANES), half),
            pltpu.VMEM((mine, members, rows, LANES), half),
            pltpu.VMEM((mine, members, rows, LANES), half),
            pltpu.VMEM((bands, members, members), half),
            pltpu.VMEM((blocks, rows, LANES), jnp.float32),
            pltpu.VMEM((members * rows, LANES), jnp.float32),
            pltpu.VMEM((members * rows, LANES), jnp.float32),
            pltpu.VMEM((1, blocks), jnp.int32),
            pltpu.VMEM((1, blocks), jnp.int32),
            pltpu.SMEM((1, blocks), jnp.int32),
            pltpu.SemaphoreType.DMA((6,)),
            pltpu.SemaphoreType.DMA((3,)),
            pltpu.SemaphoreType.DMA,
            pltpu.SemaphoreType.DMA((mine,)),
            pltpu.SemaphoreType.DMA((2,)),
            pltpu.SemaphoreType.REGULAR,
        ],
        compiler_params=pltpu.CompilerParams(
            collective_id=0, has_side_effects=True, vmem_limit_bytes=58 * 2**20
        ),
        name="exchange",
    )(block_device.reshape(1, blocks), tiled, weights[0], control)
    steps = 8
    analysis = pl.pallas_call(
        place,
        out_shape=jax.ShapeDtypeStruct((blocks, local, rows, LANES), half),
        in_specs=[smem, any_space],
        out_specs=any_space,
        scratch_shapes=[pltpu.SemaphoreType.DMA],
        compiler_params=pltpu.CompilerParams(vmem_limit_bytes=8 * 2**20),
        name="place",
    )(block_device, returned)
    return (
        analysis.reshape(blocks, local, pieces, band_rows, LANES)
        .transpose(0, 1, 3, 2, 4)
        .reshape(blocks, local, band_rows, width)
    )


def solution(mesh):
    return jax.shard_map(
        functools.partial(per_device, mesh.shape["member"], mesh.shape["patch"]),
        mesh=mesh,
        in_specs=(
            P(None, "member", "patch", None),
            P(),
            P(("member", "patch"), None, None, None),
            P(None, "patch", None),
        ),
        out_specs=P(None, "member", "patch", None),
        check_vma=False,
    )
```

```python
import functools

import jax
import jax.numpy as jnp
from jax import lax
from jax.experimental import pallas as pl
from jax.experimental.pallas import tpu as pltpu
from jax.sharding import PartitionSpec as P

RELAXATION = 0.85
EPSILON = 1e-06
MESH = pl.DeviceIdType.MESH
LANES = 128


def wait_bytes(ref, sem):
    pltpu.make_async_copy(ref, ref, sem).wait()


def analyse(gathered, transform, control, pert, moved, result, members, rows):
    zero = jnp.zeros((rows, LANES), jnp.float32)

    def add(k, total):
        return total + gathered[k].astype(jnp.float32)

    prior_mean = lax.fori_loop(0, members, add, zero, unroll=8) / members

    def perturb(k, total):
        value = gathered[k].astype(jnp.float32) - prior_mean
        pert[pl.ds(pl.multiple_of(k * rows, rows), rows), :] = value
        return total + value * value

    prior_spread = lax.fori_loop(0, members, perturb, zero, unroll=8) / members

    out_in = transform.astype(jnp.float32).T.astype(jnp.bfloat16)
    for s in range(0, rows, 2):
        both = jnp.concatenate(
            [pert[pl.ds(s + i, members, stride=rows), :].astype(jnp.bfloat16) for i in range(2)],
            axis=1,
        )
        product = jnp.dot(out_in, both, preferred_element_type=jnp.float32)
        for i in range(2):
            moved[pl.ds(s + i, members, stride=rows), :] = product[:, i * LANES : (i + 1) * LANES]

    def at(j):
        return moved[pl.ds(pl.multiple_of(j * rows, rows), rows), :]

    post_mean = lax.fori_loop(0, members, lambda j, t: t + at(j), zero, unroll=8) / members

    def square(j, total):
        centered = at(j) - post_mean
        return total + centered * centered

    posterior_spread = lax.fori_loop(0, members, square, zero, unroll=8) / members
    factor = RELAXATION * jnp.sqrt((prior_spread + EPSILON) / (posterior_spread + EPSILON)) + (
        1.0 - RELAXATION
    )

    def write(j, carry):
        member = (prior_mean + factor * (at(j) - post_mean)).astype(jnp.bfloat16)
        result[j] = (member.astype(jnp.float32) + control).astype(jnp.bfloat16)
        return carry

    lax.fori_loop(0, members, write, 0, unroll=8)


def exchange(
    groups, bands, patches,
    block_device, fields, weights, control,
    returned,
    held, ordered, gathered, result, chosen, increments, pert, moved, devices, owner_row, owners,
    load_sems, weight_sems, gather_send, gather_recv, return_sems, later,
):
    blocks, local, rows, _ = held.shape
    mine = blocks // groups
    members = groups * local
    group = lax.axis_index("member")
    band = lax.axis_index("patch")
    parts = 4

    def load_fields(i):
        part = pl.ds(i * (blocks // parts), blocks // parts)
        return pltpu.make_async_copy(fields.at[part], held.at[part], load_sems.at[2 + i])

    load_control = pltpu.make_async_copy(control, increments, load_sems.at[0])

    def other_group(i):
        return lax.rem(group + i, groups)

    def half(of_band):
        return lax.rem(of_band // 2, 2)

    def weights_peer(to):
        return group // 2 * 2 + lax.rem(group + half(band) + half(to), 2), to

    def slot_of(to, i):
        return (to // 2 * 2 + lax.rem(to + half(band) + half(i), 2)) * bands + i

    barrier = pltpu.get_barrier_semaphore()

    def greet_group(i, carry):
        pl.semaphore_signal(barrier, inc=1, device_id=(other_group(i), band), device_id_type=MESH)
        return carry

    def greet_later(to, carry):
        pl.semaphore_signal(barrier, inc=1, device_id=weights_peer(to), device_id_type=MESH)
        return carry

    def greet_earlier(to, carry):
        pl.semaphore_signal(later, inc=1, device_id=weights_peer(to), device_id_type=MESH)
        return carry

    lax.fori_loop(1, groups, greet_group, 0)
    load_devices = pltpu.make_async_copy(block_device, devices, load_sems.at[1])
    load_devices.start()
    for i in range(parts):
        load_fields(i).start()
    lax.fori_loop(band + 1, bands, greet_later, 0)

    load_devices.wait()
    shape = (blocks, blocks)
    match = devices[...] == lax.broadcasted_iota(jnp.int32, shape, 0)
    index = jnp.where(match, lax.broadcasted_iota(jnp.int32, shape, 1), 0)
    owner_row[...] = jnp.max(index.T, axis=0, keepdims=True)
    load_owners = pltpu.make_async_copy(owner_row, owners, load_sems.at[1])
    load_owners.start()

    pl.semaphore_wait(barrier, groups - 1 + band)

    per_patch = bands // patches

    def send_weights(to, carry):
        pltpu.make_async_remote_copy(
            src_ref=weights.at[to // per_patch],
            dst_ref=chosen.at[band],
            send_sem=weight_sems.at[0],
            recv_sem=weight_sems.at[1],
            device_id=weights_peer(to),
            device_id_type=MESH,
        ).start()
        return carry

    own_weights = pltpu.make_async_copy(
        weights.at[band // per_patch], chosen.at[band], weight_sems.at[2]
    )
    own_weights.start()

    load_owners.wait()
    for i in range(parts):
        load_fields(i).wait()
    load_control.start()

    def send_block(c, carry):
        here = owners[0, slot_of(group, c)]
        for k in range(local):
            gathered[c, group * local + k] = held[here, k]

        def to_peer(i, inner):
            to = other_group(i)
            block = owners[0, slot_of(to, c)]
            for k in range(local):
                ordered[i - 1, c, k] = held[block, k]
            pltpu.make_async_remote_copy(
                src_ref=ordered.at[i - 1, c],
                dst_ref=gathered.at[c, pl.ds(group * local, local)],
                send_sem=gather_send,
                recv_sem=gather_recv.at[c],
                device_id=(to, band),
                device_id_type=MESH,
            ).start()
            return inner

        lax.fori_loop(1, groups, to_peer, 0)
        return carry

    lax.fori_loop(0, 1, send_block, 0)
    lax.fori_loop(0, band, greet_earlier, 0)
    lax.fori_loop(0, band, send_weights, 0)
    lax.fori_loop(1, 2, send_block, 0)

    @pl.when(band < bands - 1)
    def _():
        pl.semaphore_wait(later, bands - 1 - band)

    lax.fori_loop(band + 1, bands, send_weights, 0)
    lax.fori_loop(2, mine, send_block, 0)

    load_control.wait()
    own_weights.wait()
    wait_bytes(chosen.at[pl.ds(0, bands - 1)], weight_sems.at[1])

    def analyse_block(c, carry):
        wait_bytes(gathered.at[c, pl.ds(0, members - local)], gather_recv.at[c])
        slot = slot_of(group, c)
        analyse(
            gathered.at[c], chosen[c], increments[owners[0, slot]],
            pert, moved, result.at[c], members, rows,
        )

        def to_peer(i, inner):
            to = other_group(i)
            pltpu.make_async_remote_copy(
                src_ref=result.at[c, pl.ds(to * local, local)],
                dst_ref=returned.at[slot],
                send_sem=return_sems.at[0],
                recv_sem=return_sems.at[1],
                device_id=(to, band),
                device_id_type=MESH,
            ).start()
            return inner

        lax.fori_loop(1, groups, to_peer, 0)
        for k in range(local):
            returned[slot, k] = result[c, group * local + k]
        return carry

    lax.fori_loop(0, mine, analyse_block, 0)

    sent = returned.at[pl.ds(0, blocks - mine)]
    wait_bytes(sent, return_sems.at[1])
    wait_bytes(chosen.at[pl.ds(0, bands - 1)], weight_sems.at[0])
    wait_bytes(ordered, gather_send)
    wait_bytes(sent, return_sems.at[0])


def place(block_device, returned, analysis, sem):
    devices = block_device[...]
    for b in range(returned.shape[0]):
        pltpu.make_async_copy(returned.at[devices[0, b]], analysis.at[b], sem).start()
    wait_bytes(returned, sem)


def per_device(groups, bands, fields, block_device, weights, control_increment):
    blocks, local, band_rows, width = fields.shape
    patches, members = weights.shape[1], weights.shape[2]
    pieces = width // LANES
    rows = pieces * band_rows
    tiled = (
        fields.reshape(blocks, local, band_rows, pieces, LANES)
        .transpose(0, 1, 3, 2, 4)
        .reshape(blocks, local, rows, LANES)
    )
    control = (
        control_increment.reshape(blocks, band_rows, pieces, LANES)
        .transpose(0, 2, 1, 3)
        .reshape(blocks, rows, LANES)
    )
    mine = blocks // groups
    any_space = pl.BlockSpec(memory_space=pl.ANY)
    smem = pl.BlockSpec(memory_space=pltpu.SMEM)
    half = jnp.bfloat16
    returned = pl.pallas_call(
        functools.partial(exchange, groups, bands, patches),
        out_shape=pltpu.VMEM((blocks, local, rows, LANES), half),
        in_specs=[pl.BlockSpec(memory_space=pltpu.HBM)] * 4,
        out_specs=pl.BlockSpec(memory_space=pltpu.VMEM),
        scratch_shapes=[
            pltpu.VMEM((blocks, local, rows, LANES), half),
            pltpu.VMEM((groups - 1, mine, local, rows, LANES), half),
            pltpu.VMEM((mine, members, rows, LANES), half),
            pltpu.VMEM((mine, members, rows, LANES), half),
            pltpu.VMEM((bands, members, members), half),
            pltpu.VMEM((blocks, rows, LANES), jnp.float32),
            pltpu.VMEM((members * rows, LANES), jnp.float32),
            pltpu.VMEM((members * rows, LANES), jnp.float32),
            pltpu.VMEM((1, blocks), jnp.int32),
            pltpu.VMEM((1, blocks), jnp.int32),
            pltpu.SMEM((1, blocks), jnp.int32),
            pltpu.SemaphoreType.DMA((6,)),
            pltpu.SemaphoreType.DMA((3,)),
            pltpu.SemaphoreType.DMA,
            pltpu.SemaphoreType.DMA((mine,)),
            pltpu.SemaphoreType.DMA((2,)),
            pltpu.SemaphoreType.REGULAR,
        ],
        compiler_params=pltpu.CompilerParams(
            collective_id=0, has_side_effects=True, vmem_limit_bytes=58 * 2**20
        ),
        name="exchange",
    )(block_device.reshape(1, blocks), tiled, weights[0], control)
    steps = 8
    analysis = pl.pallas_call(
        place,
        out_shape=jax.ShapeDtypeStruct((blocks, local, rows, LANES), half),
        in_specs=[pl.BlockSpec(memory_space=pltpu.VMEM), any_space],
        out_specs=any_space,
        scratch_shapes=[pltpu.SemaphoreType.DMA],
        compiler_params=pltpu.CompilerParams(vmem_limit_bytes=8 * 2**20),
        name="place",
    )(block_device.reshape(1, blocks), returned)
    return (
        analysis.reshape(blocks, local, pieces, band_rows, LANES)
        .transpose(0, 1, 3, 2, 4)
        .reshape(blocks, local, band_rows, width)
    )


def solution(mesh):
    return jax.shard_map(
        functools.partial(per_device, mesh.shape["member"], mesh.shape["patch"]),
        mesh=mesh,
        in_specs=(
            P(None, "member", "patch", None),
            P(),
            P(("member", "patch"), None, None, None),
            P(None, "patch", None),
        ),
        out_specs=P(None, "member", "patch", None),
        check_vma=False,
    )
```

```python
import functools

import jax
import jax.numpy as jnp
from jax import lax
from jax.experimental import pallas as pl
from jax.experimental.pallas import tpu as pltpu
from jax.sharding import PartitionSpec as P

RELAXATION = 0.85
EPSILON = 1e-06
MESH = pl.DeviceIdType.MESH
LANES = 128


def wait_bytes(ref, sem):
    pltpu.make_async_copy(ref, ref, sem).wait()


def analyse(gathered, transform, control, pert, moved, result, members, rows):
    zero = jnp.zeros((rows, LANES), jnp.float32)

    def add(k, total):
        return total + gathered[k].astype(jnp.float32)

    prior_mean = lax.fori_loop(0, members, add, zero, unroll=8) / members

    def perturb(k, total):
        value = gathered[k].astype(jnp.float32) - prior_mean
        pert[pl.ds(pl.multiple_of(k * rows, rows), rows), :] = value
        return total + value * value

    prior_spread = lax.fori_loop(0, members, perturb, zero, unroll=8) / members

    out_in = transform.astype(jnp.float32).T.astype(jnp.bfloat16)
    for s in range(0, rows, 2):
        both = jnp.concatenate(
            [pert[pl.ds(s + i, members, stride=rows), :].astype(jnp.bfloat16) for i in range(2)],
            axis=1,
        )
        product = jnp.dot(out_in, both, preferred_element_type=jnp.float32)
        for i in range(2):
            moved[pl.ds(s + i, members, stride=rows), :] = product[:, i * LANES : (i + 1) * LANES]

    def at(j):
        return moved[pl.ds(pl.multiple_of(j * rows, rows), rows), :]

    post_mean = lax.fori_loop(0, members, lambda j, t: t + at(j), zero, unroll=8) / members

    def square(j, total):
        centered = at(j) - post_mean
        return total + centered * centered

    posterior_spread = lax.fori_loop(0, members, square, zero, unroll=8) / members
    factor = RELAXATION * jnp.sqrt((prior_spread + EPSILON) / (posterior_spread + EPSILON)) + (
        1.0 - RELAXATION
    )

    def write(j, carry):
        member = (prior_mean + factor * (at(j) - post_mean)).astype(jnp.bfloat16)
        result[j] = (member.astype(jnp.float32) + control).astype(jnp.bfloat16)
        return carry

    lax.fori_loop(0, members, write, 0, unroll=8)


def exchange(
    groups, bands, patches,
    block_device, fields, weights, control,
    returned,
    held, held_rest, ordered, gathered, result, chosen, increments, pert, moved, devices, owner_row, owners,
    load_sems, weight_sems, gather_send, gather_recv, return_sems, later,
):
    blocks, local, rows, _ = fields.shape
    mine = blocks // groups
    members = groups * local
    group = lax.axis_index("member")
    band = lax.axis_index("patch")
    parts = 2
    early = held.shape[1]

    def load_fields(i, rest):
        part = pl.ds(i * (blocks // parts), blocks // parts)
        some = pl.ds(early, local - early) if rest else pl.ds(0, early)
        return pltpu.make_async_copy(
            fields.at[part, some],
            (held_rest if rest else held).at[part],
            load_sems.at[2 + i + (parts if rest else 0)],
        )

    def member(block, k):
        return held[block, k] if k < early else held_rest[block, k - early]

    load_control = pltpu.make_async_copy(control, increments, load_sems.at[0])

    def other_group(i):
        return lax.rem(group + i, groups)

    def half(of_band):
        return lax.rem(of_band // 2, 2)

    def weights_peer(to):
        return group // 2 * 2 + lax.rem(group + half(band) + half(to), 2), to

    def slot_of(to, i):
        return (to // 2 * 2 + lax.rem(to + half(band) + half(i), 2)) * bands + i

    barrier = pltpu.get_barrier_semaphore()

    def greet_group(i, carry):
        pl.semaphore_signal(barrier, inc=1, device_id=(other_group(i), band), device_id_type=MESH)
        return carry

    def place_in_order(of_band):
        return of_band // 2 * 2 + 1 - lax.rem(of_band, 2)

    rank = place_in_order(band)

    def greet_later(i, carry):
        to = place_in_order(i)
        pl.semaphore_signal(barrier, inc=1, device_id=weights_peer(to), device_id_type=MESH)
        return carry

    def greet_earlier(i, carry):
        to = place_in_order(i)
        pl.semaphore_signal(later, inc=1, device_id=weights_peer(to), device_id_type=MESH)
        return carry

    lax.fori_loop(1, groups, greet_group, 0)
    load_devices = pltpu.make_async_copy(block_device, devices, load_sems.at[1])
    load_devices.start()
    for i in range(parts):
        load_fields(i, False).start()
    for i in range(parts):
        load_fields(i, True).start()
    lax.fori_loop(rank + 1, bands, greet_later, 0)

    load_devices.wait()
    shape = (blocks, blocks)
    match = devices[...] == lax.broadcasted_iota(jnp.int32, shape, 0)
    index = jnp.where(match, lax.broadcasted_iota(jnp.int32, shape, 1), 0)
    owner_row[...] = jnp.max(index.T, axis=0, keepdims=True)
    load_owners = pltpu.make_async_copy(owner_row, owners, load_sems.at[1])
    load_owners.start()

    pl.semaphore_wait(barrier, groups - 1 + rank)

    per_patch = bands // patches

    def send_weights(i, carry):
        to = place_in_order(i)
        pltpu.make_async_remote_copy(
            src_ref=weights.at[to // per_patch],
            dst_ref=chosen.at[band],
            send_sem=weight_sems.at[0],
            recv_sem=weight_sems.at[1],
            device_id=weights_peer(to),
            device_id_type=MESH,
        ).start()
        return carry

    own_weights = pltpu.make_async_copy(
        weights.at[band // per_patch], chosen.at[band], weight_sems.at[2]
    )
    own_weights.start()

    load_owners.wait()
    for i in range(parts):
        load_fields(i, False).wait()

    def send_block(c, carry, first=0, last=local):
        here = owners[0, slot_of(group, c)]
        for k in range(first, last):
            gathered[c, group * local + k] = member(here, k)

        def to_peer(i, inner):
            to = other_group(i)
            block = owners[0, slot_of(to, c)]
            for k in range(first, last):
                ordered[i - 1, c, k] = member(block, k)
            pltpu.make_async_remote_copy(
                src_ref=ordered.at[i - 1, c, pl.ds(first, last - first)],
                dst_ref=gathered.at[c, pl.ds(group * local + first, last - first)],
                send_sem=gather_send,
                recv_sem=gather_recv.at[c],
                device_id=(to, band),
                device_id_type=MESH,
            ).start()
            return inner

        lax.fori_loop(1, groups, to_peer, 0)
        return carry

    send_block(0, 0, last=early)
    for i in range(parts):
        load_fields(i, True).wait()
    load_control.start()
    send_block(0, 0, first=early)
    lax.fori_loop(1, 4, send_block, 0)
    lax.fori_loop(0, rank, greet_earlier, 0)
    lax.fori_loop(0, rank, send_weights, 0)
    lax.fori_loop(4, 5, send_block, 0)

    @pl.when(rank < bands - 1)
    def _():
        pl.semaphore_wait(later, bands - 1 - rank)

    lax.fori_loop(rank + 1, bands, send_weights, 0)
    lax.fori_loop(5, mine, send_block, 0)

    load_control.wait()
    own_weights.wait()
    wait_bytes(chosen.at[pl.ds(0, bands - 1)], weight_sems.at[1])

    def analyse_block(c, carry):
        wait_bytes(gathered.at[c, pl.ds(0, members - local)], gather_recv.at[c])
        slot = slot_of(group, c)
        analyse(
            gathered.at[c], chosen[c], increments[owners[0, slot]],
            pert, moved, result.at[c], members, rows,
        )

        def to_peer(i, inner):
            to = other_group(i)
            pltpu.make_async_remote_copy(
                src_ref=result.at[c, pl.ds(to * local, local)],
                dst_ref=returned.at[slot],
                send_sem=return_sems.at[0],
                recv_sem=return_sems.at[1],
                device_id=(to, band),
                device_id_type=MESH,
            ).start()
            return inner

        lax.fori_loop(1, groups, to_peer, 0)
        for k in range(local):
            returned[slot, k] = result[c, group * local + k]
        return carry

    lax.fori_loop(0, mine, analyse_block, 0)

    sent = returned.at[pl.ds(0, blocks - mine)]
    wait_bytes(sent, return_sems.at[1])
    wait_bytes(chosen.at[pl.ds(0, bands - 1)], weight_sems.at[0])
    wait_bytes(ordered, gather_send)
    wait_bytes(sent, return_sems.at[0])


def place(block_device, returned, analysis, sem):
    devices = block_device[...]
    for b in range(returned.shape[0]):
        pltpu.make_async_copy(returned.at[devices[0, b]], analysis.at[b], sem).start()
    wait_bytes(returned, sem)


def per_device(groups, bands, fields, block_device, weights, control_increment):
    blocks, local, band_rows, width = fields.shape
    patches, members = weights.shape[1], weights.shape[2]
    pieces = width // LANES
    rows = pieces * band_rows
    tiled = (
        fields.reshape(blocks, local, band_rows, pieces, LANES)
        .transpose(0, 1, 3, 2, 4)
        .reshape(blocks, local, rows, LANES)
    )
    control = (
        control_increment.reshape(blocks, band_rows, pieces, LANES)
        .transpose(0, 2, 1, 3)
        .reshape(blocks, rows, LANES)
    )
    mine = blocks // groups
    early = local // 2
    any_space = pl.BlockSpec(memory_space=pl.ANY)
    smem = pl.BlockSpec(memory_space=pltpu.SMEM)
    half = jnp.bfloat16
    returned = pl.pallas_call(
        functools.partial(exchange, groups, bands, patches),
        out_shape=pltpu.VMEM((blocks, local, rows, LANES), half),
        in_specs=[pl.BlockSpec(memory_space=pltpu.HBM)] * 4,
        out_specs=pl.BlockSpec(memory_space=pltpu.VMEM),
        scratch_shapes=[
            pltpu.VMEM((blocks, early, rows, LANES), half),
            pltpu.VMEM((blocks, local - early, rows, LANES), half),
            pltpu.VMEM((groups - 1, mine, local, rows, LANES), half),
            pltpu.VMEM((mine, members, rows, LANES), half),
            pltpu.VMEM((mine, members, rows, LANES), half),
            pltpu.VMEM((bands, members, members), half),
            pltpu.VMEM((blocks, rows, LANES), jnp.float32),
            pltpu.VMEM((members * rows + rows, LANES), jnp.float32),
            pltpu.VMEM((members * rows + rows, LANES), jnp.float32),
            pltpu.VMEM((1, blocks), jnp.int32),
            pltpu.VMEM((1, blocks), jnp.int32),
            pltpu.SMEM((1, blocks), jnp.int32),
            pltpu.SemaphoreType.DMA((6,)),
            pltpu.SemaphoreType.DMA((3,)),
            pltpu.SemaphoreType.DMA,
            pltpu.SemaphoreType.DMA((mine,)),
            pltpu.SemaphoreType.DMA((2,)),
            pltpu.SemaphoreType.REGULAR,
        ],
        compiler_params=pltpu.CompilerParams(
            collective_id=0, has_side_effects=True, vmem_limit_bytes=58 * 2**20
        ),
        name="exchange",
    )(block_device.reshape(1, blocks), tiled, weights[0], control)
    steps = 8
    analysis = pl.pallas_call(
        place,
        out_shape=jax.ShapeDtypeStruct((blocks, local, rows, LANES), half),
        in_specs=[pl.BlockSpec(memory_space=pltpu.VMEM), any_space],
        out_specs=any_space,
        scratch_shapes=[pltpu.SemaphoreType.DMA],
        compiler_params=pltpu.CompilerParams(vmem_limit_bytes=8 * 2**20),
        name="place",
    )(block_device.reshape(1, blocks), returned)
    return (
        analysis.reshape(blocks, local, pieces, band_rows, LANES)
        .transpose(0, 1, 3, 2, 4)
        .reshape(blocks, local, band_rows, width)
    )


def solution(mesh):
    return jax.shard_map(
        functools.partial(per_device, mesh.shape["member"], mesh.shape["patch"]),
        mesh=mesh,
        in_specs=(
            P(None, "member", "patch", None),
            P(),
            P(("member", "patch"), None, None, None),
            P(None, "patch", None),
        ),
        out_specs=P(None, "member", "patch", None),
        check_vma=False,
    )
```

```python
import functools

import jax
import jax.numpy as jnp
from jax import lax
from jax.experimental import pallas as pl
from jax.experimental.pallas import tpu as pltpu
from jax.sharding import PartitionSpec as P

RELAXATION = 0.85
EPSILON = 1e-06
MESH = pl.DeviceIdType.MESH
AHEAD = 8
LANES = 128


def wait_bytes(ref, sem):
    pltpu.make_async_copy(ref, ref, sem).wait()


def analyse(gathered, transform, control, pert, moved, result, members, rows):
    zero = jnp.zeros((rows, LANES), jnp.float32)

    def add(k, total):
        return total + gathered[k].astype(jnp.float32)

    prior_mean = lax.fori_loop(0, members, add, zero, unroll=8) / members

    def perturb(k, total):
        value = gathered[k].astype(jnp.float32) - prior_mean
        pert[pl.ds(pl.multiple_of(k * rows, rows), rows), :] = value
        return total + value * value

    prior_spread = lax.fori_loop(0, members, perturb, zero, unroll=8) / members

    out_in = transform.astype(jnp.float32).T.astype(jnp.bfloat16)
    for s in range(0, rows, 2):
        both = jnp.concatenate(
            [pert[pl.ds(s + i, members, stride=rows), :].astype(jnp.bfloat16) for i in range(2)],
            axis=1,
        )
        product = jnp.dot(out_in, both, preferred_element_type=jnp.float32)
        for i in range(2):
            moved[pl.ds(s + i, members, stride=rows), :] = product[:, i * LANES : (i + 1) * LANES]

    def at(j):
        return moved[pl.ds(pl.multiple_of(j * rows, rows), rows), :]

    post_mean = lax.fori_loop(0, members, lambda j, t: t + at(j), zero, unroll=8) / members

    def square(j, total):
        centered = at(j) - post_mean
        return total + centered * centered

    posterior_spread = lax.fori_loop(0, members, square, zero, unroll=8) / members
    factor = RELAXATION * jnp.sqrt((prior_spread + EPSILON) / (posterior_spread + EPSILON)) + (
        1.0 - RELAXATION
    )

    def write(j, carry):
        member = (prior_mean + factor * (at(j) - post_mean)).astype(jnp.bfloat16)
        result[j] = (member.astype(jnp.float32) + control).astype(jnp.bfloat16)
        return carry

    lax.fori_loop(0, members, write, 0, unroll=8)


def exchange(
    groups, bands, patches,
    block_device, fields, weights, control,
    returned,
    held, held_rest, ordered, gathered, result, chosen, increments, pert, moved, devices, owner_row, owners,
    load_sems, weight_sems, gather_send, gather_recv, return_sems, later,
):
    blocks, local, rows, _ = fields.shape
    mine = blocks // groups
    members = groups * local
    group = lax.axis_index("member")
    band = lax.axis_index("patch")
    parts = 2
    early = held.shape[1]

    def load_fields(i, rest):
        part = pl.ds(i * (blocks // parts), blocks // parts)
        some = pl.ds(early, local - early) if rest else pl.ds(0, early)
        return pltpu.make_async_copy(
            fields.at[part, some],
            (held_rest if rest else held).at[part],
            load_sems.at[2 + i + (parts if rest else 0)],
        )

    def member(block, k):
        return held[block, k] if k < early else held_rest[block, k - early]

    load_control = pltpu.make_async_copy(control, increments, load_sems.at[0])

    def other_group(i):
        return lax.rem(group + i, groups)

    def half(of_band):
        return lax.rem(of_band // 2, 2)

    def weights_peer(to):
        return group // 2 * 2 + lax.rem(group + half(band) + half(to), 2), to

    def slot_of(to, i):
        return (to // 2 * 2 + lax.rem(to + half(band) + half(i), 2)) * bands + i

    barrier = pltpu.get_barrier_semaphore()

    def greet_group(i, carry):
        pl.semaphore_signal(barrier, inc=1, device_id=(other_group(i), band), device_id_type=MESH)
        return carry

    def place_in_order(of_band):
        return of_band // 2 * 2 + 1 - lax.rem(of_band, 2)

    rank = place_in_order(band)

    def greet_later(i, carry):
        to = place_in_order(i)
        pl.semaphore_signal(barrier, inc=1, device_id=weights_peer(to), device_id_type=MESH)
        return carry

    def greet_earlier(i, carry):
        to = place_in_order(i)
        pl.semaphore_signal(later, inc=1, device_id=weights_peer(to), device_id_type=MESH)
        return carry

    lax.fori_loop(1, groups, greet_group, 0)
    load_devices = pltpu.make_async_copy(block_device, devices, load_sems.at[1])
    load_devices.start()
    for i in range(parts):
        load_fields(i, False).start()
    for i in range(parts):
        load_fields(i, True).start()
    lax.fori_loop(rank + 1, bands, greet_later, 0)

    load_devices.wait()
    shape = (blocks, blocks)
    match = devices[...] == lax.broadcasted_iota(jnp.int32, shape, 0)
    index = jnp.where(match, lax.broadcasted_iota(jnp.int32, shape, 1), 0)
    owner_row[...] = jnp.max(index.T, axis=0, keepdims=True)
    load_owners = pltpu.make_async_copy(owner_row, owners, load_sems.at[1])
    load_owners.start()

    pl.semaphore_wait(barrier, groups - 1 + rank)

    per_patch = bands // patches

    def send_weights(i, carry):
        to = place_in_order(i)
        pltpu.make_async_remote_copy(
            src_ref=weights.at[to // per_patch],
            dst_ref=chosen.at[band],
            send_sem=weight_sems.at[0],
            recv_sem=weight_sems.at[1],
            device_id=weights_peer(to),
            device_id_type=MESH,
        ).start()
        return carry

    own_weights = pltpu.make_async_copy(
        weights.at[band // per_patch], chosen.at[band], weight_sems.at[2]
    )
    own_weights.start()

    load_owners.wait()
    for i in range(parts):
        load_fields(i, False).wait()

    def send_block(c, carry, first=0, last=local):
        here = owners[0, slot_of(group, c)]
        for k in range(first, last):
            gathered[c, group * local + k] = member(here, k)

        def to_peer(i, inner):
            to = other_group(i)
            block = owners[0, slot_of(to, c)]
            for k in range(first, last):
                ordered[i - 1, c, k] = member(block, k)
            pltpu.make_async_remote_copy(
                src_ref=ordered.at[i - 1, c, pl.ds(first, last - first)],
                dst_ref=gathered.at[c, pl.ds(group * local + first, last - first)],
                send_sem=gather_send,
                recv_sem=gather_recv.at[c],
                device_id=(to, band),
                device_id_type=MESH,
            ).start()
            return inner

        lax.fori_loop(1, groups, to_peer, 0)
        return carry

    send_block(0, 0, last=early)
    for i in range(parts):
        load_fields(i, True).wait()
    load_control.start()
    send_block(0, 0, first=early)
    lax.fori_loop(1, 4, send_block, 0)
    lax.fori_loop(0, rank, greet_earlier, 0)
    lax.fori_loop(0, rank, send_weights, 0)
    lax.fori_loop(4, 5, send_block, 0)

    @pl.when(rank < bands - 1)
    def _():
        pl.semaphore_wait(later, bands - 1 - rank)

    lax.fori_loop(rank + 1, bands, send_weights, 0)
    lax.fori_loop(5, AHEAD, send_block, 0)

    load_control.wait()
    own_weights.wait()
    wait_bytes(chosen.at[pl.ds(0, bands - 1)], weight_sems.at[1])

    def analyse_block(c, carry):
        wait_bytes(gathered.at[c, pl.ds(0, members - local)], gather_recv.at[c])
        slot = slot_of(group, c)
        analyse(
            gathered.at[c], chosen[c], increments[owners[0, slot]],
            pert, moved, result.at[c], members, rows,
        )

        def to_peer(i, inner):
            to = other_group(i)
            pltpu.make_async_remote_copy(
                src_ref=result.at[c, pl.ds(to * local, local)],
                dst_ref=returned.at[slot],
                send_sem=return_sems.at[0],
                recv_sem=return_sems.at[1],
                device_id=(to, band),
                device_id_type=MESH,
            ).start()
            return inner

        lax.fori_loop(1, groups, to_peer, 0)
        @pl.when(c + AHEAD < mine)
        def _():
            send_block(c + AHEAD, 0)

        for k in range(local):
            returned[slot, k] = result[c, group * local + k]
        return carry

    lax.fori_loop(0, mine, analyse_block, 0)

    sent = returned.at[pl.ds(0, blocks - mine)]
    wait_bytes(sent, return_sems.at[1])
    wait_bytes(chosen.at[pl.ds(0, bands - 1)], weight_sems.at[0])
    wait_bytes(ordered, gather_send)
    wait_bytes(sent, return_sems.at[0])


def place(block_device, returned, analysis, sem):
    devices = block_device[...]
    for b in range(returned.shape[0]):
        pltpu.make_async_copy(returned.at[devices[0, b]], analysis.at[b], sem).start()
    wait_bytes(returned, sem)


def per_device(groups, bands, fields, block_device, weights, control_increment):
    blocks, local, band_rows, width = fields.shape
    patches, members = weights.shape[1], weights.shape[2]
    pieces = width // LANES
    rows = pieces * band_rows
    tiled = (
        fields.reshape(blocks, local, band_rows, pieces, LANES)
        .transpose(0, 1, 3, 2, 4)
        .reshape(blocks, local, rows, LANES)
    )
    control = (
        control_increment.reshape(blocks, band_rows, pieces, LANES)
        .transpose(0, 2, 1, 3)
        .reshape(blocks, rows, LANES)
    )
    mine = blocks // groups
    early = local // 2
    any_space = pl.BlockSpec(memory_space=pl.ANY)
    smem = pl.BlockSpec(memory_space=pltpu.SMEM)
    half = jnp.bfloat16
    returned = pl.pallas_call(
        functools.partial(exchange, groups, bands, patches),
        out_shape=pltpu.VMEM((blocks, local, rows, LANES), half),
        in_specs=[pl.BlockSpec(memory_space=pltpu.HBM)] * 4,
        out_specs=pl.BlockSpec(memory_space=pltpu.VMEM),
        scratch_shapes=[
            pltpu.VMEM((blocks, early, rows, LANES), half),
            pltpu.VMEM((blocks, local - early, rows, LANES), half),
            pltpu.VMEM((groups - 1, mine, local, rows, LANES), half),
            pltpu.VMEM((mine, members, rows, LANES), half),
            pltpu.VMEM((mine, members, rows, LANES), half),
            pltpu.VMEM((bands, members, members), half),
            pltpu.VMEM((blocks, rows, LANES), jnp.float32),
            pltpu.VMEM((members * rows + rows, LANES), jnp.float32),
            pltpu.VMEM((members * rows + rows, LANES), jnp.float32),
            pltpu.VMEM((1, blocks), jnp.int32),
            pltpu.VMEM((1, blocks), jnp.int32),
            pltpu.SMEM((1, blocks), jnp.int32),
            pltpu.SemaphoreType.DMA((6,)),
            pltpu.SemaphoreType.DMA((3,)),
            pltpu.SemaphoreType.DMA,
            pltpu.SemaphoreType.DMA((mine,)),
            pltpu.SemaphoreType.DMA((2,)),
            pltpu.SemaphoreType.REGULAR,
        ],
        compiler_params=pltpu.CompilerParams(
            collective_id=0, has_side_effects=True, vmem_limit_bytes=58 * 2**20
        ),
        name="exchange",
    )(block_device.reshape(1, blocks), tiled, weights[0], control)
    steps = 8
    analysis = pl.pallas_call(
        place,
        out_shape=jax.ShapeDtypeStruct((blocks, local, rows, LANES), half),
        in_specs=[pl.BlockSpec(memory_space=pltpu.VMEM), any_space],
        out_specs=any_space,
        scratch_shapes=[pltpu.SemaphoreType.DMA],
        compiler_params=pltpu.CompilerParams(vmem_limit_bytes=8 * 2**20),
        name="place",
    )(block_device.reshape(1, blocks), returned)
    return (
        analysis.reshape(blocks, local, pieces, band_rows, LANES)
        .transpose(0, 1, 3, 2, 4)
        .reshape(blocks, local, band_rows, width)
    )


def solution(mesh):
    return jax.shard_map(
        functools.partial(per_device, mesh.shape["member"], mesh.shape["patch"]),
        mesh=mesh,
        in_specs=(
            P(None, "member", "patch", None),
            P(),
            P(("member", "patch"), None, None, None),
            P(None, "patch", None),
        ),
        out_specs=P(None, "member", "patch", None),
        check_vma=False,
    )
```

```python
import functools

import jax
import jax.numpy as jnp
from jax import lax
from jax.experimental import pallas as pl
from jax.experimental.pallas import tpu as pltpu
from jax.sharding import PartitionSpec as P

RELAXATION = 0.85
EPSILON = 1e-06
MESH = pl.DeviceIdType.MESH
AHEAD = 8
HELD = 4
LATE = 6
LANES = 128


def wait_bytes(ref, sem):
    pltpu.make_async_copy(ref, ref, sem).wait()


def analyse(gathered, transform, control, pert, moved, result, members, rows):
    zero = jnp.zeros((rows, LANES), jnp.float32)

    def add(k, total):
        return total + gathered[k].astype(jnp.float32)

    prior_mean = lax.fori_loop(0, members, add, zero, unroll=8) / members

    def perturb(k, total):
        value = gathered[k].astype(jnp.float32) - prior_mean
        pert[pl.ds(pl.multiple_of(k * rows, rows), rows), :] = value
        return total + value * value

    prior_spread = lax.fori_loop(0, members, perturb, zero, unroll=8) / members

    out_in = transform.astype(jnp.float32).T.astype(jnp.bfloat16)
    for s in range(0, rows, 2):
        both = jnp.concatenate(
            [pert[pl.ds(s + i, members, stride=rows), :].astype(jnp.bfloat16) for i in range(2)],
            axis=1,
        )
        product = jnp.dot(out_in, both, preferred_element_type=jnp.float32)
        for i in range(2):
            moved[pl.ds(s + i, members, stride=rows), :] = product[:, i * LANES : (i + 1) * LANES]

    def at(j):
        return moved[pl.ds(pl.multiple_of(j * rows, rows), rows), :]

    post_mean = lax.fori_loop(0, members, lambda j, t: t + at(j), zero, unroll=8) / members

    def square(j, total):
        centered = at(j) - post_mean
        return total + centered * centered

    posterior_spread = lax.fori_loop(0, members, square, zero, unroll=8) / members
    factor = RELAXATION * jnp.sqrt((prior_spread + EPSILON) / (posterior_spread + EPSILON)) + (
        1.0 - RELAXATION
    )

    def write(j, carry):
        member = (prior_mean + factor * (at(j) - post_mean)).astype(jnp.bfloat16)
        result[j] = (member.astype(jnp.float32) + control).astype(jnp.bfloat16)
        return carry

    lax.fori_loop(0, members, write, 0, unroll=8)


def exchange(
    groups, bands, patches,
    block_device, fields, weights, control,
    returned,
    held, held_rest, ordered, gathered, result, chosen, increments, pert, moved, devices, owner_row, owners,
    load_sems, weight_sems, gather_send, gather_recv, return_sems, later,
):
    blocks, local, rows, _ = fields.shape
    mine = blocks // groups
    members = groups * local
    group = lax.axis_index("member")
    band = lax.axis_index("patch")
    parts = 2
    early = held.shape[1]

    def load_fields(i, rest):
        part = pl.ds(i * (blocks // parts), blocks // parts)
        some = pl.ds(early, local - early) if rest else pl.ds(0, early)
        return pltpu.make_async_copy(
            fields.at[part, some],
            (held_rest if rest else held).at[part],
            load_sems.at[2 + i + (parts if rest else 0)],
        )

    def member(block, k):
        return held[block, k] if k < early else held_rest[block, k - early]

    load_control = pltpu.make_async_copy(control, increments, load_sems.at[0])

    def other_group(i):
        return lax.rem(group + i, groups)

    def half(of_band):
        return lax.rem(of_band // 2, 2)

    def weights_peer(to):
        return group // 2 * 2 + lax.rem(group + half(band) + half(to), 2), to

    def slot_of(to, i):
        return (to // 2 * 2 + lax.rem(to + half(band) + half(i), 2)) * bands + i

    barrier = pltpu.get_barrier_semaphore()

    def greet_group(i, carry):
        pl.semaphore_signal(barrier, inc=1, device_id=(other_group(i), band), device_id_type=MESH)
        return carry

    def place_in_order(of_band):
        return of_band // 2 * 2 + 1 - lax.rem(of_band, 2)

    rank = place_in_order(band)

    def greet_later(i, carry):
        to = place_in_order(i)
        pl.semaphore_signal(barrier, inc=1, device_id=weights_peer(to), device_id_type=MESH)
        return carry

    def greet_earlier(i, carry):
        to = place_in_order(i)
        pl.semaphore_signal(later, inc=1, device_id=weights_peer(to), device_id_type=MESH)
        return carry

    lax.fori_loop(1, groups, greet_group, 0)
    load_devices = pltpu.make_async_copy(block_device, devices, load_sems.at[1])
    load_devices.start()
    for i in range(parts):
        load_fields(i, False).start()
    for i in range(parts):
        load_fields(i, True).start()
    lax.fori_loop(rank + 1, bands, greet_later, 0)

    load_devices.wait()
    shape = (blocks, blocks)
    match = devices[...] == lax.broadcasted_iota(jnp.int32, shape, 0)
    index = jnp.where(match, lax.broadcasted_iota(jnp.int32, shape, 1), 0)
    owner_row[...] = jnp.max(index.T, axis=0, keepdims=True)
    load_owners = pltpu.make_async_copy(owner_row, owners, load_sems.at[1])
    load_owners.start()

    pl.semaphore_wait(barrier, groups - 1 + rank)

    per_patch = bands // patches

    def send_weights(i, carry):
        to = place_in_order(i)
        pltpu.make_async_remote_copy(
            src_ref=weights.at[to // per_patch],
            dst_ref=chosen.at[band],
            send_sem=weight_sems.at[0],
            recv_sem=weight_sems.at[1],
            device_id=weights_peer(to),
            device_id_type=MESH,
        ).start()
        return carry

    own_weights = pltpu.make_async_copy(
        weights.at[band // per_patch], chosen.at[band], weight_sems.at[2]
    )
    own_weights.start()

    load_owners.wait()
    for i in range(parts):
        load_fields(i, False).wait()

    def send_block(c, carry, first=0, last=local):
        here = owners[0, slot_of(group, c)]
        for k in range(first, last):
            gathered[c, group * local + k] = member(here, k)

        def to_peer(i, inner):
            to = other_group(i)
            block = owners[0, slot_of(to, c)]
            for k in range(first, last):
                ordered[i - 1, c, k] = member(block, k)
            pltpu.make_async_remote_copy(
                src_ref=ordered.at[i - 1, c, pl.ds(first, last - first)],
                dst_ref=gathered.at[c, pl.ds(group * local + first, last - first)],
                send_sem=gather_send,
                recv_sem=gather_recv.at[c],
                device_id=(to, band),
                device_id_type=MESH,
            ).start()
            return inner

        lax.fori_loop(1, groups, to_peer, 0)
        return carry

    send_block(0, 0, last=early)
    for i in range(parts):
        load_fields(i, True).wait()
    load_control.start()
    send_block(0, 0, first=early)
    lax.fori_loop(1, 4, send_block, 0)
    lax.fori_loop(0, rank, greet_earlier, 0)
    lax.fori_loop(0, rank, send_weights, 0)
    lax.fori_loop(4, 5, send_block, 0)

    @pl.when(rank < bands - 1)
    def _():
        pl.semaphore_wait(later, bands - 1 - rank)

    lax.fori_loop(rank + 1, bands, send_weights, 0)
    lax.fori_loop(5, AHEAD, send_block, 0)

    load_control.wait()
    own_weights.wait()
    wait_bytes(chosen.at[pl.ds(0, bands - 1)], weight_sems.at[1])

    def send_back(c, to):
        pltpu.make_async_remote_copy(
            src_ref=result.at[c, pl.ds(to * local, local)],
            dst_ref=returned.at[slot_of(group, c)],
            send_sem=return_sems.at[0],
            recv_sem=return_sems.at[1],
            device_id=(to, band),
            device_id_type=MESH,
        ).start()

    def held_back(to):
        return (group >= LATE) & (to >= LATE)

    def analyse_block(c, carry):
        wait_bytes(gathered.at[c, pl.ds(0, members - local)], gather_recv.at[c])
        slot = slot_of(group, c)
        analyse(
            gathered.at[c], chosen[c], increments[owners[0, slot]],
            pert, moved, result.at[c], members, rows,
        )

        def to_peer(i, inner):
            to = other_group(i)
            block = jnp.where(held_back(to), c - HELD, c)

            @pl.when(block >= 0)
            def _():
                send_back(block, to)

            return inner

        lax.fori_loop(1, groups, to_peer, 0)
        @pl.when(c + AHEAD < mine)
        def _():
            send_block(c + AHEAD, 0)

        for k in range(local):
            returned[slot, k] = result[c, group * local + k]
        return carry

    lax.fori_loop(0, mine, analyse_block, 0)

    def send_last(i, carry):
        to = other_group(i)

        @pl.when(held_back(to))
        def _():
            for c in range(mine - HELD, mine):
                send_back(c, to)

        return carry

    lax.fori_loop(1, groups, send_last, 0)

    sent = returned.at[pl.ds(0, blocks - mine)]
    wait_bytes(sent, return_sems.at[1])
    wait_bytes(chosen.at[pl.ds(0, bands - 1)], weight_sems.at[0])
    wait_bytes(ordered, gather_send)
    wait_bytes(sent, return_sems.at[0])


def place(block_device, returned, analysis, sem):
    devices = block_device[...]
    for b in range(returned.shape[0]):
        pltpu.make_async_copy(returned.at[devices[0, b]], analysis.at[b], sem).start()
    wait_bytes(returned, sem)


def per_device(groups, bands, fields, block_device, weights, control_increment):
    blocks, local, band_rows, width = fields.shape
    patches, members = weights.shape[1], weights.shape[2]
    pieces = width // LANES
    rows = pieces * band_rows
    tiled = (
        fields.reshape(blocks, local, band_rows, pieces, LANES)
        .transpose(0, 1, 3, 2, 4)
        .reshape(blocks, local, rows, LANES)
    )
    control = (
        control_increment.reshape(blocks, band_rows, pieces, LANES)
        .transpose(0, 2, 1, 3)
        .reshape(blocks, rows, LANES)
    )
    mine = blocks // groups
    early = local // 2
    any_space = pl.BlockSpec(memory_space=pl.ANY)
    smem = pl.BlockSpec(memory_space=pltpu.SMEM)
    half = jnp.bfloat16
    returned = pl.pallas_call(
        functools.partial(exchange, groups, bands, patches),
        out_shape=pltpu.VMEM((blocks, local, rows, LANES), half),
        in_specs=[pl.BlockSpec(memory_space=pltpu.HBM)] * 4,
        out_specs=pl.BlockSpec(memory_space=pltpu.VMEM),
        scratch_shapes=[
            pltpu.VMEM((blocks, early, rows, LANES), half),
            pltpu.VMEM((blocks, local - early, rows, LANES), half),
            pltpu.VMEM((groups - 1, mine, local, rows, LANES), half),
            pltpu.VMEM((mine, members, rows, LANES), half),
            pltpu.VMEM((mine, members, rows, LANES), half),
            pltpu.VMEM((bands, members, members), half),
            pltpu.VMEM((blocks, rows, LANES), jnp.float32),
            pltpu.VMEM((members * rows + rows, LANES), jnp.float32),
            pltpu.VMEM((members * rows + rows, LANES), jnp.float32),
            pltpu.VMEM((1, blocks), jnp.int32),
            pltpu.VMEM((1, blocks), jnp.int32),
            pltpu.SMEM((1, blocks), jnp.int32),
            pltpu.SemaphoreType.DMA((6,)),
            pltpu.SemaphoreType.DMA((3,)),
            pltpu.SemaphoreType.DMA,
            pltpu.SemaphoreType.DMA((mine,)),
            pltpu.SemaphoreType.DMA((2,)),
            pltpu.SemaphoreType.REGULAR,
        ],
        compiler_params=pltpu.CompilerParams(
            collective_id=0, has_side_effects=True, vmem_limit_bytes=58 * 2**20
        ),
        name="exchange",
    )(block_device.reshape(1, blocks), tiled, weights[0], control)
    steps = 8
    analysis = pl.pallas_call(
        place,
        out_shape=jax.ShapeDtypeStruct((blocks, local, rows, LANES), half),
        in_specs=[pl.BlockSpec(memory_space=pltpu.VMEM), any_space],
        out_specs=any_space,
        scratch_shapes=[pltpu.SemaphoreType.DMA],
        compiler_params=pltpu.CompilerParams(vmem_limit_bytes=8 * 2**20),
        name="place",
    )(block_device.reshape(1, blocks), returned)
    return (
        analysis.reshape(blocks, local, pieces, band_rows, LANES)
        .transpose(0, 1, 3, 2, 4)
        .reshape(blocks, local, band_rows, width)
    )


def solution(mesh):
    return jax.shard_map(
        functools.partial(per_device, mesh.shape["member"], mesh.shape["patch"]),
        mesh=mesh,
        in_specs=(
            P(None, "member", "patch", None),
            P(),
            P(("member", "patch"), None, None, None),
            P(None, "patch", None),
        ),
        out_specs=P(None, "member", "patch", None),
        check_vma=False,
    )
```

```python
import functools

import jax
import jax.numpy as jnp
from jax import lax
from jax.experimental import pallas as pl
from jax.experimental.pallas import tpu as pltpu
from jax.sharding import PartitionSpec as P

RELAXATION = 0.85
EPSILON = 1e-06
MESH = pl.DeviceIdType.MESH
AHEAD = 8
LANES = 128


def wait_bytes(ref, sem):
    pltpu.make_async_copy(ref, ref, sem).wait()


def analyse(gathered, transform, control, pert, moved, result, members, rows):
    zero = jnp.zeros((rows, LANES), jnp.float32)

    def add(k, total):
        return total + gathered[k].astype(jnp.float32)

    prior_mean = lax.fori_loop(0, members, add, zero, unroll=8) / members

    def perturb(k, total):
        value = gathered[k].astype(jnp.float32) - prior_mean
        pert[pl.ds(pl.multiple_of(k * rows, rows), rows), :] = value
        return total + value * value

    prior_spread = lax.fori_loop(0, members, perturb, zero, unroll=8) / members

    out_in = transform.astype(jnp.float32).T.astype(jnp.bfloat16)
    for s in range(0, rows, 2):
        both = jnp.concatenate(
            [pert[pl.ds(s + i, members, stride=rows), :].astype(jnp.bfloat16) for i in range(2)],
            axis=1,
        )
        product = jnp.dot(out_in, both, preferred_element_type=jnp.float32)
        for i in range(2):
            moved[pl.ds(s + i, members, stride=rows), :] = product[:, i * LANES : (i + 1) * LANES]

    def at(j):
        return moved[pl.ds(pl.multiple_of(j * rows, rows), rows), :]

    post_mean = lax.fori_loop(0, members, lambda j, t: t + at(j), zero, unroll=8) / members

    def square(j, total):
        centered = at(j) - post_mean
        return total + centered * centered

    posterior_spread = lax.fori_loop(0, members, square, zero, unroll=8) / members
    factor = RELAXATION * jnp.sqrt((prior_spread + EPSILON) / (posterior_spread + EPSILON)) + (
        1.0 - RELAXATION
    )

    def write(j, carry):
        member = (prior_mean + factor * (at(j) - post_mean)).astype(jnp.bfloat16)
        result[j] = (member.astype(jnp.float32) + control).astype(jnp.bfloat16)
        return carry

    lax.fori_loop(0, members, write, 0, unroll=8)


def exchange(
    groups, bands, patches,
    block_device, fields, weights, control,
    returned,
    held, held_rest, ordered, gathered, result, chosen, increments, pert, moved, devices, owner_row, owners,
    load_sems, weight_sems, gather_send, gather_recv, return_sems, later,
):
    blocks, local, rows, _ = fields.shape
    mine = blocks // groups
    members = groups * local
    group = lax.axis_index("member")
    band = lax.axis_index("patch")
    parts = 2
    early = held.shape[1]

    def load_fields(i, rest):
        part = pl.ds(i * (blocks // parts), blocks // parts)
        some = pl.ds(early, local - early) if rest else pl.ds(0, early)
        return pltpu.make_async_copy(
            fields.at[part, some],
            (held_rest if rest else held).at[part],
            load_sems.at[2 + i + (parts if rest else 0)],
        )

    def member(block, k):
        return held[block, k] if k < early else held_rest[block, k - early]

    load_control = pltpu.make_async_copy(control, increments, load_sems.at[0])

    def other_group(i):
        return lax.rem(group + i, groups)

    def half(of_band):
        return lax.rem(of_band // 2, 2)

    def weights_peer(to):
        return group // 2 * 2 + lax.rem(group + half(band) + half(to), 2), to

    def slot_of(to, i):
        return (to // 2 * 2 + lax.rem(to + half(band) + half(i), 2)) * bands + i

    barrier = pltpu.get_barrier_semaphore()

    def greet_group(i, carry):
        pl.semaphore_signal(barrier, inc=1, device_id=(other_group(i), band), device_id_type=MESH)
        return carry

    def place_in_order(of_band):
        return of_band // 2 * 2 + 1 - lax.rem(of_band, 2)

    rank = place_in_order(band)

    def greet_later(i, carry):
        to = place_in_order(i)
        pl.semaphore_signal(barrier, inc=1, device_id=weights_peer(to), device_id_type=MESH)
        return carry

    def greet_earlier(i, carry):
        to = place_in_order(i)
        pl.semaphore_signal(later, inc=1, device_id=weights_peer(to), device_id_type=MESH)
        return carry

    lax.fori_loop(1, groups, greet_group, 0)
    load_devices = pltpu.make_async_copy(block_device, devices, load_sems.at[1])
    load_devices.start()
    for i in range(parts):
        load_fields(i, False).start()
    for i in range(parts):
        load_fields(i, True).start()
    lax.fori_loop(rank + 1, bands, greet_later, 0)

    load_devices.wait()
    shape = (blocks, blocks)
    match = devices[...] == lax.broadcasted_iota(jnp.int32, shape, 0)
    index = jnp.where(match, lax.broadcasted_iota(jnp.int32, shape, 1), 0)
    owner_row[...] = jnp.max(index.T, axis=0, keepdims=True)
    load_owners = pltpu.make_async_copy(owner_row, owners, load_sems.at[1])
    load_owners.start()

    pl.semaphore_wait(barrier, groups - 1 + rank)

    per_patch = bands // patches

    def send_weights(i, carry):
        to = place_in_order(i)
        pltpu.make_async_remote_copy(
            src_ref=weights.at[to // per_patch],
            dst_ref=chosen.at[band],
            send_sem=weight_sems.at[0],
            recv_sem=weight_sems.at[1],
            device_id=weights_peer(to),
            device_id_type=MESH,
        ).start()
        return carry

    own_weights = pltpu.make_async_copy(
        weights.at[band // per_patch], chosen.at[band], weight_sems.at[2]
    )
    own_weights.start()

    load_owners.wait()
    for i in range(parts):
        load_fields(i, False).wait()

    def send_block(c, carry, first=0, last=local):
        here = owners[0, slot_of(group, c)]
        for k in range(first, last):
            gathered[c, group * local + k] = member(here, k)

        def to_peer(i, inner):
            to = other_group(i)
            block = owners[0, slot_of(to, c)]
            for k in range(first, last):
                ordered[i - 1, c, k] = member(block, k)
            pltpu.make_async_remote_copy(
                src_ref=ordered.at[i - 1, c, pl.ds(first, last - first)],
                dst_ref=gathered.at[c, pl.ds(group * local + first, last - first)],
                send_sem=gather_send,
                recv_sem=gather_recv.at[c],
                device_id=(to, band),
                device_id_type=MESH,
            ).start()
            return inner

        lax.fori_loop(1, groups, to_peer, 0)
        return carry

    send_block(0, 0, last=early)
    for i in range(parts):
        load_fields(i, True).wait()
    load_control.start()
    send_block(0, 0, first=early)
    lax.fori_loop(1, 4, send_block, 0)
    lax.fori_loop(0, rank, greet_earlier, 0)
    lax.fori_loop(0, rank, send_weights, 0)
    lax.fori_loop(4, 5, send_block, 0)

    @pl.when(rank < bands - 1)
    def _():
        pl.semaphore_wait(later, bands - 1 - rank)

    lax.fori_loop(rank + 1, bands, send_weights, 0)
    lax.fori_loop(5, AHEAD, send_block, 0)

    load_control.wait()
    own_weights.wait()
    wait_bytes(chosen.at[pl.ds(0, bands - 1)], weight_sems.at[1])

    def analyse_block(c, carry):
        wait_bytes(gathered.at[c, pl.ds(0, members - local)], gather_recv.at[c])
        slot = slot_of(group, c)
        analyse(
            gathered.at[c], chosen[c], increments[owners[0, slot]],
            pert, moved, result.at[c], members, rows,
        )

        def to_peer(i, inner):
            to = other_group(i)
            pltpu.make_async_remote_copy(
                src_ref=result.at[c, pl.ds(to * local, local)],
                dst_ref=returned.at[slot],
                send_sem=return_sems.at[0],
                recv_sem=return_sems.at[1],
                device_id=(to, band),
                device_id_type=MESH,
            ).start()
            return inner

        lax.fori_loop(1, groups, to_peer, 0)
        @pl.when(c + AHEAD < mine)
        def _():
            send_block(c + AHEAD, 0)

        for k in range(local):
            returned[slot, k] = result[c, group * local + k]
        return carry

    lax.fori_loop(0, mine, analyse_block, 0)

    sent = returned.at[pl.ds(0, blocks - mine)]
    wait_bytes(sent, return_sems.at[1])
    wait_bytes(chosen.at[pl.ds(0, bands - 1)], weight_sems.at[0])
    wait_bytes(ordered, gather_send)
    wait_bytes(sent, return_sems.at[0])


def place(block_device, returned, analysis, sem):
    devices = block_device[...]
    for b in range(returned.shape[0]):
        pltpu.make_async_copy(returned.at[devices[0, b]], analysis.at[b], sem).start()
    wait_bytes(returned, sem)


def per_device(groups, bands, fields, block_device, weights, control_increment):
    blocks, local, band_rows, width = fields.shape
    patches, members = weights.shape[1], weights.shape[2]
    pieces = width // LANES
    rows = pieces * band_rows
    tiled = (
        fields.reshape(blocks, local, band_rows, pieces, LANES)
        .transpose(0, 1, 3, 2, 4)
        .reshape(blocks, local, rows, LANES)
    )
    control = (
        control_increment.reshape(blocks, band_rows, pieces, LANES)
        .transpose(0, 2, 1, 3)
        .reshape(blocks, rows, LANES)
    )
    mine = blocks // groups
    early = max(1, local // 5)
    any_space = pl.BlockSpec(memory_space=pl.ANY)
    smem = pl.BlockSpec(memory_space=pltpu.SMEM)
    half = jnp.bfloat16
    returned = pl.pallas_call(
        functools.partial(exchange, groups, bands, patches),
        out_shape=pltpu.VMEM((blocks, local, rows, LANES), half),
        in_specs=[pl.BlockSpec(memory_space=pltpu.HBM)] * 4,
        out_specs=pl.BlockSpec(memory_space=pltpu.VMEM),
        scratch_shapes=[
            pltpu.VMEM((blocks, early, rows, LANES), half),
            pltpu.VMEM((blocks, local - early, rows, LANES), half),
            pltpu.VMEM((groups - 1, mine, local, rows, LANES), half),
            pltpu.VMEM((mine, members, rows, LANES), half),
            pltpu.VMEM((mine, members, rows, LANES), half),
            pltpu.VMEM((bands, members, members), half),
            pltpu.VMEM((blocks, rows, LANES), jnp.float32),
            pltpu.VMEM((members * rows + rows, LANES), jnp.float32),
            pltpu.VMEM((members * rows + rows, LANES), jnp.float32),
            pltpu.VMEM((1, blocks), jnp.int32),
            pltpu.VMEM((1, blocks), jnp.int32),
            pltpu.SMEM((1, blocks), jnp.int32),
            pltpu.SemaphoreType.DMA((6,)),
            pltpu.SemaphoreType.DMA((3,)),
            pltpu.SemaphoreType.DMA,
            pltpu.SemaphoreType.DMA((mine,)),
            pltpu.SemaphoreType.DMA((2,)),
            pltpu.SemaphoreType.REGULAR,
        ],
        compiler_params=pltpu.CompilerParams(
            collective_id=0, has_side_effects=True, vmem_limit_bytes=58 * 2**20
        ),
        name="exchange",
    )(block_device.reshape(1, blocks), tiled, weights[0], control)
    steps = 8
    analysis = pl.pallas_call(
        place,
        out_shape=jax.ShapeDtypeStruct((blocks, local, rows, LANES), half),
        in_specs=[pl.BlockSpec(memory_space=pltpu.VMEM), any_space],
        out_specs=any_space,
        scratch_shapes=[pltpu.SemaphoreType.DMA],
        compiler_params=pltpu.CompilerParams(vmem_limit_bytes=8 * 2**20),
        name="place",
    )(block_device.reshape(1, blocks), returned)
    return (
        analysis.reshape(blocks, local, pieces, band_rows, LANES)
        .transpose(0, 1, 3, 2, 4)
        .reshape(blocks, local, band_rows, width)
    )


def solution(mesh):
    return jax.shard_map(
        functools.partial(per_device, mesh.shape["member"], mesh.shape["patch"]),
        mesh=mesh,
        in_specs=(
            P(None, "member", "patch", None),
            P(),
            P(("member", "patch"), None, None, None),
            P(None, "patch", None),
        ),
        out_specs=P(None, "member", "patch", None),
        check_vma=False,
    )
```
